32 devices in a mesh: cfg: 2 (over x), seq: 16 (over z, y, core).
Axes of the slice: x: 2, y: 2, z: 4, core: 2. Of those that a mesh axis runs over, the one named last changes fastest.
Arguments:
- img_queries: bfloat16 [2, 192, 1216], P('cfg', 'seq')
- img_keys: bfloat16 [2, 192, 1216], P('cfg', 'seq')
- img_values: bfloat16 [2, 192, 1216], P('cfg', 'seq'), may hold values from -6 to 6
- text_keys: bfloat16 [2, 16, 1216], P('cfg', 'seq'), may hold values from -6 to 6
- text_values: bfloat16 [2, 16, 1216], P('cfg', 'seq'), may hold values from -18 to 18
- query_gain: float32 [64], replicated, may hold values from 0.5 to 8, as said below
- key_gain: float32 [64], replicated, may hold values from 0.5 to 8, as said below
- text_gain: float32 [64], replicated, may hold values from 0.5 to 8, as said below
- text_lengths: int32 [2], P('cfg'), may hold values from 1 to 16, as said below
- text_blocks: int32 [2, 16], P('cfg', 'seq'), may hold values from 0 to 1
- latent: float32 [192, 64], P('seq', 'cfg'), may hold values from -6 to 6
- base_velocity: bfloat16 [2, 192, 64], P('cfg', 'seq'), may hold values from -6 to 6
- out_weight: bfloat16 [1216, 64], replicated, may hold values from -1.25 to 1.25
- timestep: int32 [1], replicated, may hold values from 0 to 27
Outputs:
- next_latent: float32 [192, 64], P('seq', 'cfg')
- denoised: float32 [192, 64], P('seq', 'cfg')
The draws below stay inside these ranges and needn't reach their ends.
Inputs may be any that keep to these rules, and one draw needn't show every extreme that they name: `query_gain`: gains are positive. `key_gain`: gains are positive. `text_gain`: gains are positive. `text_lengths`: one of the two halves has all 16 slots within its length.
All inputs are finite; a program needn't handle non-finite values.
Results may differ from the reference program's by a relative error of at most 0.007.
The reference program's roundings to bfloat16 on the way count: a program that leaves them out, or rounds other values in their place, can miss the bound.
Values may be sent and summed in bfloat16 or wider, within the bound.
A program may use at most 128 MiB of HBM per device.

```python
import math
import jax
import jax.numpy as jnp
from jax import lax

HEADS = 19
D_HEAD = 64
CH = 64
TXT_DEV = 1
STEPS = 28
IMG = 192
TXT = 16


def pair_tokens(key):
    width = HEADS * D_HEAD
    base_queries = jax.random.normal(jax.random.fold_in(key, 101), (2, IMG, width), jnp.float32)
    base_keys = jax.random.normal(jax.random.fold_in(key, 202), (2, IMG, width), jnp.float32)
    return (base_queries, base_keys)


def draw_img_queries(key, part):
    return pair_tokens(key)[0].astype(jnp.bfloat16)


def draw_img_keys(key, part):
    return pair_tokens(key)[1].astype(jnp.bfloat16)


def gain_vector(key, salt):
    sub_key = jax.random.fold_in(key, salt)
    return jnp.exp(jax.random.uniform(sub_key, (D_HEAD,), jnp.float32, minval=math.log(0.5), maxval=math.log(2.0)))


def draw_query_gain(key, part):
    return gain_vector(key, 11)


def draw_key_gain(key, part):
    return gain_vector(key, 12)


def draw_text_gain(key, part):
    return gain_vector(key, 13)


def draw_text_lengths(key, part):
    drawn = jax.random.randint(jax.random.fold_in(key, 55), (2,), 1, TXT + 1, dtype=jnp.int32)
    full_half = jax.random.randint(jax.random.fold_in(key, 56), (), 0, 2, dtype=jnp.int32)
    halves = jnp.arange(2, dtype=jnp.int32)
    return jnp.where(halves == full_half, jnp.int32(TXT), drawn).astype(jnp.int32)


def draw_text_blocks(key, part):
    levels = jax.random.randint(jax.random.fold_in(key, 66), (2, TXT // TXT_DEV), 0, 4, dtype=jnp.int32)
    return (levels > 0).astype(jnp.int32)


def level_of(rng, shape, split, smallest, top_value):
    level = 1.0
    for dim, blocks in split:
        draws = jax.random.uniform(jax.random.fold_in(jax.random.fold_in(rng, 6), dim), (blocks,), jnp.float32, smallest / len(split), top_value / len(split))
        level = level * jnp.repeat(jnp.exp(draws), shape[dim] // blocks).reshape((-1,) + (1,) * (len(shape) - 1 - dim))
    return level


def bell_draw(stream_key, shape, deviation, limit, pieces=(), kind=jnp.bfloat16):
    loudness = level_of(stream_key, shape, pieces, -0.22, 0.18) if pieces else 1.0
    values = jax.random.normal(stream_key, shape, jnp.float32) * deviation * loudness
    return jnp.minimum(jnp.maximum(values, -limit), limit).astype(kind)


def setup_inputs(seed: int = 0) -> dict:
    arg_keys = jax.random.split(jax.random.key(seed), 15)
    img_queries = draw_img_queries(jax.random.fold_in(arg_keys[14], 71), 0)
    img_keys = draw_img_keys(jax.random.fold_in(arg_keys[14], 71), 0)
    img_values = bell_draw(arg_keys[2], (2, IMG, HEADS * D_HEAD), 1.0, 6.0, ((0, 2), (1, 16)))
    text_keys = bell_draw(arg_keys[3], (2, TXT, HEADS * D_HEAD), 1.0, 6.0, ((0, 2), (1, 16)))
    text_values = bell_draw(arg_keys[4], (2, TXT, HEADS * D_HEAD), 3.0, 18.0, ((0, 2), (1, 16)))
    query_gain = draw_query_gain(jax.random.fold_in(arg_keys[14], 71), 0)
    key_gain = draw_key_gain(jax.random.fold_in(arg_keys[14], 71), 0)
    text_gain = draw_text_gain(jax.random.fold_in(arg_keys[14], 71), 0)
    text_lengths = draw_text_lengths(jax.random.fold_in(arg_keys[14], 71), 0)
    text_blocks = draw_text_blocks(jax.random.fold_in(arg_keys[14], 71), 0)
    latent = bell_draw(arg_keys[10], (IMG, CH), 1.0, 6.0, ((0, 16), (1, 2)), jnp.float32)
    base_velocity = bell_draw(arg_keys[11], (2, IMG, CH), 1.0, 6.0, ((0, 2), (1, 16)))
    out_weight = bell_draw(arg_keys[12], (HEADS * D_HEAD, CH), (HEADS * D_HEAD // 64) ** -0.5, 1.25)
    timestep = jax.random.randint(arg_keys[13], (1,), 0, STEPS).astype(jnp.int32)
    return dict(img_queries=img_queries, img_keys=img_keys, img_values=img_values, text_keys=text_keys, text_values=text_values, query_gain=query_gain, key_gain=key_gain, text_gain=text_gain, text_lengths=text_lengths, text_blocks=text_blocks, latent=latent, base_velocity=base_velocity, out_weight=out_weight, timestep=timestep)


epsilon = 1e-06
guidance = 3.5
shift_factor = 3.0
masked_score = -1e+30

def head_norm(values, gain_row):
    widened = values.astype(jnp.float32).reshape(values.shape[0], -1, gain_row.shape[0])
    scaled = widened * lax.rsqrt(lax.optimization_barrier(jnp.mean(widened * widened, axis=-1, keepdims=True)) + epsilon) * gain_row
    return scaled.astype(jnp.bfloat16)

def sigma_at(position):
    time_left = 1.0 - position / STEPS
    return shift_factor * time_left / (1.0 + (shift_factor - 1.0) * time_left)

def attend_half(queries, keys_image, values_image, keys_text, values_text, usable):
    head_size = queries.shape[2]
    scale = 1.0 / math.sqrt(head_size)
    keys_all = jnp.concatenate([keys_image, keys_text], axis=0)
    values_all = jnp.concatenate([values_image.reshape(values_image.shape[0], -1, head_size), values_text.reshape(values_text.shape[0], -1, head_size)], axis=0)
    valid = jnp.concatenate([jnp.ones((keys_image.shape[0],), dtype=jnp.bool_), usable])

    def one_head(head_input):
        query_head, key_head, value_head = head_input
        scores = jnp.dot(query_head, key_head.T, preferred_element_type=jnp.float32) * scale
        scores = jnp.where(valid[None, :], scores, masked_score)
        row_top = lax.optimization_barrier(jnp.max(scores, axis=-1, keepdims=True))
        exponent = jnp.where(valid[None, :], jnp.exp(scores - row_top), 0.0)
        row_total = lax.optimization_barrier(jnp.sum(exponent, axis=-1))
        summed = jnp.dot(exponent.astype(jnp.bfloat16), value_head, preferred_element_type=jnp.float32)
        return summed / row_total[:, None]
    per_head = lax.map(one_head, (queries.transpose(1, 0, 2), keys_all.transpose(1, 0, 2), values_all.transpose(1, 0, 2)))
    return per_head.transpose(1, 0, 2).reshape(queries.shape[0], -1).astype(jnp.bfloat16)

def reference(img_queries, img_keys, img_values, text_keys, text_values, query_gain, key_gain, text_gain, text_lengths, text_blocks, latent, base_velocity, out_weight, timestep):
    slots = jnp.arange(TXT, dtype=jnp.int32)
    velocities = []
    for guide_half in range(2):
        queries = head_norm(img_queries[guide_half], query_gain)
        keys_image = head_norm(img_keys[guide_half], key_gain)
        keys_text = head_norm(text_keys[guide_half], text_gain)
        block_flag = text_blocks[guide_half][slots // TXT_DEV]
        usable = (slots < text_lengths[guide_half]) & (block_flag == 1)
        attended = attend_half(queries, keys_image, img_values[guide_half], keys_text, text_values[guide_half], usable)
        velocity = base_velocity[guide_half].astype(jnp.float32) + jnp.dot(attended, out_weight, preferred_element_type=jnp.float32)
        velocities.append(velocity)
    guided = velocities[1] + guidance * (velocities[0] - velocities[1])
    step_now = timestep[0].astype(jnp.float32)
    sigma_now = sigma_at(step_now)
    sigma_next = sigma_at(step_now + 1.0)
    next_latent = latent + (sigma_next - sigma_now) * guided
    denoised = latent - sigma_now * guided
    return (next_latent, denoised)
```

```python
import functools
import math

import jax
import jax.numpy as jnp
from jax import lax
from jax.experimental import pallas as pl
from jax.experimental.pallas import tpu as pltpu
from jax.sharding import PartitionSpec as P

STEPS = 28
MESH = pl.DeviceIdType.MESH

epsilon = 1e-06
guidance = 3.5
shift_factor = 3.0
masked_score = -1e30

SLOT_ROWS = 16
PACK = 4


def sigma_at(position):
    time_left = 1.0 - position / STEPS
    return shift_factor * time_left / (1.0 + (shift_factor - 1.0) * time_left)


def exchange_kernel(
    plan,
    q_hbm, k_hbm, v_hbm, tk_hbm, tv_hbm, gq_ref, gk_ref, gt_ref, len_ref, blk_ref, base_hbm, w_hbm,
    out_ref,
    q_in, k_in, v_in, tk_in, tv_in, base_in, w_in,
    stage, recv, packed, wide, parts, recv2,
    load_sem, send_sem, recv_sem, send2_sem, recv2_sem,
):
    n, group, heads, head_size, rows, texts, half = plan
    extras = heads - group
    f32, bf16 = jnp.float32, jnp.bfloat16
    cfg = lax.axis_index("cfg")
    me = lax.axis_index("seq")
    place = lax.rem(me, group)
    first = me - place
    row_groups = rows // PACK

    def extra_of(position):
        step = position - group // 4
        index = lax.div(step, 3)
        has = (step >= 0) & (lax.rem(step, 3) == 0) & (index < extras)
        return has, group + jnp.clip(index, 0, extras - 1)

    has_extra, extra_head = extra_of(place)

    loads = []
    sources = (
        (k_hbm.at[0], k_in), (tk_hbm.at[0], tk_in), (q_hbm.at[0], q_in), (v_hbm.at[0], v_in), (tv_hbm.at[0], tv_in),
        (base_hbm.at[0], base_in),
        (w_hbm.at[pl.ds(pl.multiple_of(place * head_size, head_size), head_size)], w_in.at[0]),
        (w_hbm.at[pl.ds(pl.multiple_of(extra_head * head_size, head_size), head_size)], w_in.at[1]),
    )
    for i, (src, dst) in enumerate(sources):
        load = pltpu.make_async_copy(src, dst, load_sem.at[i])
        load.start()
        loads.append(load)

    barrier = pltpu.get_barrier_semaphore()

    def greet_half(i, carry):
        peer = lax.rem(me + i, n)
        pl.semaphore_signal(barrier, inc=1, device_id=(cfg, peer), device_id_type=MESH)
        return carry

    def greet_other(i, carry):
        pl.semaphore_signal(barrier, inc=1, device_id=(1 - cfg, first + i), device_id_type=MESH)
        return carry

    lax.fori_loop(1, n, greet_half, 0)
    lax.fori_loop(0, group, greet_other, 0)

    lane = lax.broadcasted_iota(jnp.int32, (SLOT_ROWS, 128), 1)
    row = lax.broadcasted_iota(jnp.int32, (SLOT_ROWS, 128), 0)
    low = lane < head_size
    gain_q = jnp.concatenate([gq_ref[...], gq_ref[...]], axis=1) * (1.0 / math.sqrt(head_size))
    gain_k = jnp.concatenate([gk_ref[...], gk_ref[...]], axis=1)
    gain_t = jnp.concatenate([gt_ref[...], gt_ref[...]], axis=1)
    is_text = (row >= rows) & (row < rows + texts)
    gain_kt = jnp.where(is_text, gain_t, gain_k)
    slot_index = me * texts + row - rows
    open_row = (row < rows) | (is_text & (slot_index < len_ref[0]) & (blk_ref[0, 0] == 1))
    bias = jnp.where((lane == 0) & jnp.logical_not(open_row), masked_score, 0.0)

    def chunk(ref, c):
        part = ref[:, c * 128:min((c + 1) * 128, heads * head_size)].astype(f32)
        if part.shape[1] < 128:
            part = jnp.concatenate([part, jnp.zeros((part.shape[0], 128 - part.shape[1]), f32)], axis=1)
        return part

    def tall(part):
        return jnp.concatenate([part, jnp.zeros((SLOT_ROWS - part.shape[0], 128), f32)], axis=0)

    def with_text(part, text):
        if texts == 1:
            return jnp.where(row == rows, text, tall(part))
        return tall(jnp.concatenate([part, text], axis=0))

    def normed(part, gain):
        square = part * part
        left = jnp.sum(jnp.where(low, square, 0.0), axis=1, keepdims=True)
        right = jnp.sum(jnp.where(low, 0.0, square), axis=1, keepdims=True)
        mean = jnp.where(low, left, right) * (1.0 / head_size)
        return part * lax.rsqrt(mean + epsilon) * gain

    for load in loads[:5]:
        load.wait()
    for c in range((heads + 1) // 2):
        qn = normed(tall(chunk(q_in, c)), gain_q)
        kn = normed(with_text(chunk(k_in, c), chunk(tk_in, c)), gain_kt)
        vv = with_text(chunk(v_in, c), chunk(tv_in, c))
        q_turn = pltpu.roll(qn, head_size, 1)
        k_turn = pltpu.roll(kn, head_size, 1)
        v_turn = pltpu.roll(vv, head_size, 1)
        stage[2 * c, :, 0:128] = jnp.where(low, bias, k_turn).astype(bf16)
        stage[2 * c, :, 128:256] = jnp.where(low, vv, q_turn).astype(bf16)
        if 2 * c + 1 < heads:
            stage[2 * c + 1, :, 0:128] = jnp.where(low, bias, kn).astype(bf16)
            stage[2 * c + 1, :, 128:256] = jnp.where(low, v_turn, qn).astype(bf16)

    pl.semaphore_wait(barrier, n - 1 + group)

    def head_copy(peer, slot, head):
        return pltpu.make_async_remote_copy(
            src_ref=stage.at[head],
            dst_ref=recv.at[slot, me],
            send_sem=send_sem.at[slot, peer],
            recv_sem=recv_sem.at[slot],
            device_id=(cfg, peer),
            device_id_type=MESH,
        )

    def send_heads(i, carry):
        peer = lax.rem(me + i, n)
        position = lax.rem(peer, group)
        more, more_head = extra_of(position)

        @pl.when(more)
        def _():
            head_copy(peer, 1, more_head).start()

        head_copy(peer, 0, position).start()
        return carry

    lax.fori_loop(1, n, send_heads, 0)
    recv[0, me] = stage[place]

    @pl.when(has_extra)
    def _():
        recv[1, me] = stage[extra_head]

    for load in loads[5:]:
        load.wait()
    lane_w = lax.broadcasted_iota(jnp.int32, (head_size, 128), 1)
    for slot in range(2):
        weight = w_in[slot].astype(f32)
        for side in range(2):
            block = weight[:, side * half:(side + 1) * half]
            tiled = jnp.concatenate([block] * (128 // half), axis=1)
            for g in range(row_groups):
                held = jnp.where(lax.div(lane_w, half) == g, tiled, 0.0)
                wide[slot, g, 0:head_size, side * 128:(side + 1) * 128] = held.astype(bf16)
                wide[slot, g, head_size:128, side * 128:(side + 1) * 128] = jnp.zeros((128 - head_size, 128), bf16)
    base = base_in[...].astype(f32)
    base_packed = []
    for side in range(2):
        pieces = [base[g * PACK:(g + 1) * PACK, side * half:(side + 1) * half] for g in range(row_groups)]
        pieces.append(jnp.zeros((PACK, 128 - row_groups * half), f32))
        base_packed.append(jnp.concatenate(pieces, axis=1))

    lane_q = lax.broadcasted_iota(jnp.int32, (group * PACK, 128), 1)

    def whole_wait(buffer, count, sem):
        span = buffer.at[pl.ds(0, count)]
        pltpu.make_async_copy(span, span, sem).wait()

    def attend(slot):
        whole_wait(recv.at[slot], n - 1, recv_sem.at[slot])
        keys = recv[slot, :, :, 0:128].reshape(n * SLOT_ROWS, 128)
        values = recv[slot, :, :, 128:256].reshape(n * SLOT_ROWS, 128)
        for s in range(group):
            own = recv[slot, first + s, :, 128:256].astype(f32)
            for g in range(row_groups):
                packed[g, s * PACK:(s + 1) * PACK, :] = own[g * PACK:(g + 1) * PACK]
        total = None
        for g in range(row_groups):
            query = jnp.where(lane_q < head_size, jnp.where(lane_q == 0, 1.0, 0.0), packed[g]).astype(bf16)
            scores = lax.dot_general(query, keys, (((1,), (1,)), ((), ())), preferred_element_type=f32)
            top = jnp.max(scores, axis=1, keepdims=True)
            weights = jnp.exp(scores - top)
            den = jnp.sum(weights, axis=1, keepdims=True)
            num = jnp.dot(weights.astype(bf16), values, preferred_element_type=f32)
            attended = (num / den).astype(bf16)
            term = jnp.dot(attended, wide[slot, g], preferred_element_type=f32)
            total = term if total is None else total + term
        return total

    total = attend(0)
    for side in range(2):
        for s in range(group):
            parts[side, s] = total[s * PACK:(s + 1) * PACK, side * 128:(side + 1) * 128]

    @pl.when(has_extra)
    def _():
        more_total = attend(1)
        for side in range(2):
            for s in range(group):
                parts[side, s] = parts[side, s] + more_total[s * PACK:(s + 1) * PACK, side * 128:(side + 1) * 128]

    for side in range(2):
        parts[side, place] = parts[side, place] + base_packed[side]

    mine = cfg * group + place

    def part_copy(side, s):
        return pltpu.make_async_remote_copy(
            src_ref=parts.at[side, s],
            dst_ref=recv2.at[mine],
            send_sem=send2_sem.at[side * group + s],
            recv_sem=recv2_sem,
            device_id=(side, first + s),
            device_id_type=MESH,
        )

    def send_parts(i, carry):
        target = lax.rem(mine + i, 2 * group)
        part_copy(lax.div(target, group), lax.rem(target, group)).start()
        return carry

    lax.fori_loop(1, 2 * group, send_parts, 0)
    recv2[mine] = parts[cfg, place]

    def sent_heads(i, carry):
        peer = lax.rem(me + i, n)
        more, more_head = extra_of(lax.rem(peer, group))

        @pl.when(more)
        def _():
            head_copy(peer, 1, more_head).wait_send()

        head_copy(peer, 0, lax.rem(peer, group)).wait_send()
        return carry

    lax.fori_loop(1, n, sent_heads, 0)

    whole_wait(recv2, 2 * group - 1, recv2_sem)
    cond = jnp.sum(recv2[0:group], axis=0)
    uncond = jnp.sum(recv2[group:2 * group], axis=0)
    guided = uncond + guidance * (cond - uncond)
    for g in range(row_groups):
        out_ref[g * PACK:(g + 1) * PACK, :] = guided[:, g * half:(g + 1) * half]

    def sent_parts(i, carry):
        target = lax.rem(mine + i, 2 * group)
        part_copy(lax.div(target, group), lax.rem(target, group)).wait_send()
        return carry

    lax.fori_loop(1, 2 * group, sent_parts, 0)


def on_device(
    n,
    img_queries, img_keys, img_values, text_keys, text_values, query_gain, key_gain, text_gain,
    text_lengths, text_blocks, latent, base_velocity, out_weight, timestep,
):
    head_size = query_gain.shape[0]
    width = img_queries.shape[2]
    heads = width // head_size
    rows, texts = img_queries.shape[1], text_keys.shape[1]
    half = latent.shape[1]
    group = max(d for d in range(1, min(n, heads) + 1) if n % d == 0)
    plan = (n, group, heads, head_size, rows, texts, half)
    bf16, f32 = jnp.bfloat16, jnp.float32
    anywhere = pl.BlockSpec(memory_space=pl.ANY)
    vmem = pl.BlockSpec(memory_space=pltpu.VMEM)
    smem = pl.BlockSpec(memory_space=pltpu.SMEM)
    guided = pl.pallas_call(
        functools.partial(exchange_kernel, plan),
        out_shape=jax.ShapeDtypeStruct((rows, half), f32),
        in_specs=[anywhere] * 5 + [vmem] * 3 + [smem] * 2 + [anywhere] * 2,
        out_specs=vmem,
        scratch_shapes=[
            pltpu.VMEM((rows, width), bf16),
            pltpu.VMEM((rows, width), bf16),
            pltpu.VMEM((rows, width), bf16),
            pltpu.VMEM((texts, width), bf16),
            pltpu.VMEM((texts, width), bf16),
            pltpu.VMEM((rows, 2 * half), bf16),
            pltpu.VMEM((2, head_size, 2 * half), bf16),
            pltpu.VMEM((heads, SLOT_ROWS, 256), bf16),
            pltpu.VMEM((2, n, SLOT_ROWS, 256), bf16),
            pltpu.VMEM((rows // PACK, group * PACK, 128), f32),
            pltpu.VMEM((2, rows // PACK, 128, 256), bf16),
            pltpu.VMEM((2, group, PACK, 128), f32),
            pltpu.VMEM((2 * group, PACK, 128), f32),
            pltpu.SemaphoreType.DMA((8,)),
            pltpu.SemaphoreType.DMA((2, n)),
            pltpu.SemaphoreType.DMA((2,)),
            pltpu.SemaphoreType.DMA((2 * group,)),
            pltpu.SemaphoreType.DMA,
        ],
        compiler_params=pltpu.CompilerParams(
            collective_id=0, has_side_effects=True, vmem_limit_bytes=40 * 1024 * 1024
        ),
    )(
        img_queries, img_keys, img_values, text_keys, text_values,
        query_gain.reshape(1, -1), key_gain.reshape(1, -1), text_gain.reshape(1, -1),
        text_lengths, text_blocks, base_velocity, out_weight,
    )
    step_now = timestep[0].astype(f32)
    sigma_now = sigma_at(step_now)
    sigma_next = sigma_at(step_now + 1.0)
    next_latent = latent + (sigma_next - sigma_now) * guided
    denoised = latent - sigma_now * guided
    return (next_latent, denoised)


def solution(mesh):
    return jax.shard_map(
        functools.partial(on_device, mesh.shape["seq"]),
        mesh=mesh,
        in_specs=(
            P("cfg", "seq", None),
            P("cfg", "seq", None),
            P("cfg", "seq", None),
            P("cfg", "seq", None),
            P("cfg", "seq", None),
            P(),
            P(),
            P(),
            P("cfg"),
            P("cfg", "seq"),
            P("seq", "cfg"),
            P("cfg", "seq", None),
            P(),
            P(),
        ),
        out_specs=(P("seq", "cfg"), P("seq", "cfg")),
        check_vma=False,
    )
```

```python
import functools
import math

import jax
import jax.numpy as jnp
from jax import lax
from jax.experimental import pallas as pl
from jax.experimental.pallas import tpu as pltpu
from jax.sharding import PartitionSpec as P

STEPS = 28
MESH = pl.DeviceIdType.MESH

epsilon = 1e-06
guidance = 3.5
shift_factor = 3.0
masked_score = -1e30

SLOT_ROWS = 16
PACK = 4


def sigma_at(position):
    time_left = 1.0 - position / STEPS
    return shift_factor * time_left / (1.0 + (shift_factor - 1.0) * time_left)


def exchange_kernel(
    plan,
    q_hbm, k_hbm, v_hbm, tk_hbm, tv_hbm, gq_hbm, gk_hbm, gt_hbm, len_ref, blk_ref, lat_hbm, base_hbm, w_hbm, step_ref,
    next_ref, clean_ref,
    q_in, k_in, v_in, tk_in, tv_in, gq_ref, gk_ref, gt_ref, lat_in, base_in, w_in,
    stage, recv, packed, wide, parts, recv2,
    load_sem, send_sem, recv_sem, send2_sem, recv2_sem,
):
    n, group, heads, head_size, rows, texts, half = plan
    row_groups = rows // PACK
    units = (heads - group) * row_groups
    unit_start = (group - units) // 2
    blocks = n // group
    f32, bf16 = jnp.float32, jnp.bfloat16
    cfg = lax.axis_index("cfg")
    me = lax.axis_index("seq")
    place = lax.rem(me, group)
    first = me - place
    unit = place - unit_start
    has_unit = (unit >= 0) & (unit < units)
    unit = jnp.clip(unit, 0, units - 1)
    unit_head = group + lax.div(unit, row_groups)
    unit_part = lax.rem(unit, row_groups)

    def each(start, stop, body):
        if stop - start <= 32:
            for i in range(start, stop):
                body(i)
        else:
            def step(i, carry):
                body(i)
                return carry
            lax.fori_loop(start, stop, step, 0)

    def wrapped(value, size):
        return jnp.where(value >= size, value - size, value)

    loads = []
    sources = (
        (k_hbm.at[0], k_in), (tk_hbm.at[0], tk_in), (q_hbm.at[0], q_in), (v_hbm.at[0], v_in), (tv_hbm.at[0], tv_in),
        (gq_hbm, gq_ref), (gk_hbm, gk_ref), (gt_hbm, gt_ref),
        (lat_hbm, lat_in), (base_hbm.at[0], base_in), (w_hbm, w_in),
    )
    for i, (src, dst) in enumerate(sources):
        load = pltpu.make_async_copy(src, dst, load_sem.at[i])
        load.start()
        loads.append(load)

    barrier = pltpu.get_barrier_semaphore()

    def greet_half(i):
        pl.semaphore_signal(barrier, inc=1, device_id=(cfg, wrapped(me + i, n)), device_id_type=MESH)

    def greet_other(i):
        pl.semaphore_signal(barrier, inc=1, device_id=(1 - cfg, first + i), device_id_type=MESH)

    each(1, n, greet_half)
    each(0, group, greet_other)

    lane = lax.broadcasted_iota(jnp.int32, (SLOT_ROWS, 128), 1)
    row = lax.broadcasted_iota(jnp.int32, (SLOT_ROWS, 128), 0)
    low = lane < head_size
    is_text = (row >= rows) & (row < rows + texts)
    slot_index = me * texts + row - rows
    open_row = (row < rows) | (is_text & (slot_index < len_ref[0]) & (blk_ref[0, 0] == 1))
    bias = jnp.where((lane == 0) & jnp.logical_not(open_row), masked_score, 0.0)

    def chunk(ref, c):
        part = ref[:, c * 128:min((c + 1) * 128, heads * head_size)].astype(f32)
        if part.shape[1] < 128:
            part = jnp.concatenate([part, jnp.zeros((part.shape[0], 128 - part.shape[1]), f32)], axis=1)
        return part

    def tall(part):
        return jnp.concatenate([part, jnp.zeros((SLOT_ROWS - part.shape[0], 128), f32)], axis=0)

    def with_text(part, text):
        if texts == 1:
            return jnp.where(row == rows, text, tall(part))
        return tall(jnp.concatenate([part, text], axis=0))

    def normed(part, gain):
        square = part * part
        left = jnp.sum(jnp.where(low, square, 0.0), axis=1, keepdims=True)
        right = jnp.sum(jnp.where(low, 0.0, square), axis=1, keepdims=True)
        mean = jnp.where(low, left, right) * (1.0 / head_size)
        return part * lax.rsqrt(mean + epsilon) * gain

    for load in loads[:8]:
        load.wait()
    gain_q = jnp.concatenate([gq_ref[...], gq_ref[...]], axis=1) * (1.0 / math.sqrt(head_size))
    gain_k = jnp.concatenate([gk_ref[...], gk_ref[...]], axis=1)
    gain_t = jnp.concatenate([gt_ref[...], gt_ref[...]], axis=1)
    gain_kt = jnp.where(is_text, gain_t, gain_k)
    for c in range((heads + 1) // 2):
        qn = normed(tall(chunk(q_in, c)), gain_q)
        kn = normed(with_text(chunk(k_in, c), chunk(tk_in, c)), gain_kt)
        vv = with_text(chunk(v_in, c), chunk(tv_in, c))
        q_turn = pltpu.roll(qn, head_size, 1)
        k_turn = pltpu.roll(kn, head_size, 1)
        v_turn = pltpu.roll(vv, head_size, 1)
        stage[2 * c, :, 0:128] = jnp.where(low, bias, k_turn).astype(bf16)
        stage[2 * c, :, 128:256] = jnp.where(low, vv, q_turn).astype(bf16)
        if 2 * c + 1 < heads:
            stage[2 * c + 1, :, 0:128] = jnp.where(low, bias, kn).astype(bf16)
            stage[2 * c + 1, :, 128:256] = jnp.where(low, v_turn, qn).astype(bf16)

    pl.semaphore_wait(barrier, n - 1 + group)

    def send_head(peer, slot, head):
        pltpu.make_async_remote_copy(
            src_ref=stage.at[head],
            dst_ref=recv.at[slot, me],
            send_sem=send_sem.at[slot],
            recv_sem=recv_sem.at[slot],
            device_id=(cfg, peer),
            device_id_type=MESH,
        ).start()

    def send_unit(block):
        for u in range(units):
            peer = block * group + unit_start + u

            @pl.when(peer != me)
            def _():
                send_head(peer, 1, group + u // row_groups)

    def send_own(i):
        peer = wrapped(me + i, n)
        send_head(peer, 0, lax.rem(peer, group) if n > group else peer)

    each(0, blocks, send_unit)
    each(1, n, send_own)
    recv[0, me] = stage[place]

    @pl.when(has_unit)
    def _():
        recv[1, me] = stage[unit_head]

    @pl.when(jnp.logical_not(has_unit))
    def _():
        recv[1] = jnp.zeros(recv.shape[1:], bf16)

    for load in loads[8:]:
        load.wait()
    wide[...] = jnp.zeros(wide.shape, bf16)
    lane_w = lax.broadcasted_iota(jnp.int32, (2 * half, 128), 1)
    full = (heads * head_size) // 128
    for slot, head in ((0, place), (1, unit_head)):
        pair = lax.div(head, 2)
        start = pl.multiple_of(jnp.minimum(pair, full - 1) * 128, 128)
        weight = w_in[:, pl.ds(start, 128)].astype(f32)
        if full * 128 < heads * head_size:
            weight = jnp.where(pair == full, chunk(w_in, full), weight)
        weight = jnp.where(lax.rem(head, 2) == 1, pltpu.roll(weight, head_size, 1), weight)
        weight = jnp.where(lane_w < head_size, weight, 0.0).astype(bf16)
        for side in range(2):
            for g in range(row_groups):
                at = side * 128 + g * half
                wide[slot, g, at:at + half, :] = weight[side * half:(side + 1) * half]
    base = base_in[...].astype(f32)
    base_packed = []
    for side in range(2):
        pieces = [base[g * PACK:(g + 1) * PACK, side * half:(side + 1) * half] for g in range(row_groups)]
        pieces.append(jnp.zeros((PACK, 128 - row_groups * half), f32))
        base_packed.append(jnp.concatenate(pieces, axis=1))
    step_now = jnp.full((PACK, half), step_ref[0], jnp.int32).astype(f32)
    sigma_now = sigma_at(step_now)
    sigma_gain = sigma_at(step_now + 1.0) - sigma_now

    def whole_wait(buffer, count, sem):
        span = buffer.at[pl.ds(0, count)]
        pltpu.make_async_copy(span, span, sem).wait()

    whole_wait(recv.at[0], n - 1, recv_sem.at[0])

    @pl.when(has_unit)
    def _():
        whole_wait(recv.at[1], n - 1, recv_sem.at[1])

    for s in range(group):
        own = recv[0, first + s, :, 128:256].astype(f32)
        for g in range(row_groups):
            packed[g, s * PACK:(s + 1) * PACK, :] = own[g * PACK:(g + 1) * PACK]
        own = recv[1, first + s, :, 128:256].astype(f32)
        chosen = own[0:PACK]
        for g in range(1, row_groups):
            chosen = jnp.where(unit_part == g, own[g * PACK:(g + 1) * PACK], chosen)
        packed[row_groups, s * PACK:(s + 1) * PACK, :] = chosen

    lane_q = lax.broadcasted_iota(jnp.int32, (group * PACK, 128), 1)
    nt = (((1,), (1,)), ((), ()))
    total = None
    for c in range(row_groups + 1):
        slot, part = (0, c) if c < row_groups else (1, unit_part)
        keys = recv[slot, :, :, 0:128].reshape(n * SLOT_ROWS, 128)
        values = recv[slot, :, :, 128:256].reshape(n * SLOT_ROWS, 128)
        query = jnp.where(lane_q < head_size, jnp.where(lane_q == 0, 1.0, 0.0), packed[c]).astype(bf16)
        scores = lax.dot_general(query, keys, nt, preferred_element_type=f32)
        top = jnp.max(scores, axis=1, keepdims=True)
        weights = jnp.exp(scores - top)
        den = jnp.sum(weights, axis=1, keepdims=True)
        num = jnp.dot(weights.astype(bf16), values, preferred_element_type=f32)
        attended = (num / den).astype(bf16)
        term = lax.dot_general(attended, wide[slot, part], nt, preferred_element_type=f32)
        total = term if total is None else total + term
    for side in range(2):
        for s in range(group):
            parts[side, s] = total[s * PACK:(s + 1) * PACK, side * 128:(side + 1) * 128]
    for side in range(2):
        parts[side, place] = parts[side, place] + base_packed[side]

    mine = cfg * group + place

    def send_part(i):
        target = wrapped(mine + i, 2 * group)
        side = jnp.where(target >= group, 1, 0)
        s = target - side * group
        pltpu.make_async_remote_copy(
            src_ref=parts.at[side, s],
            dst_ref=recv2.at[mine],
            send_sem=send2_sem,
            recv_sem=recv2_sem,
            device_id=(side, first + s),
            device_id_type=MESH,
        ).start()

    each(1, 2 * group, send_part)
    recv2[mine] = parts[cfg, place]

    whole_wait(recv.at[0], n - 1, send_sem.at[0])

    @pl.when(has_unit)
    def _():
        whole_wait(recv.at[1], units * blocks - 1, send_sem.at[1])

    @pl.when(jnp.logical_not(has_unit))
    def _():
        whole_wait(recv.at[1], units * blocks, send_sem.at[1])

    whole_wait(recv2, 2 * group - 1, recv2_sem)
    cond = jnp.sum(recv2[0:group], axis=0)
    uncond = jnp.sum(recv2[group:2 * group], axis=0)
    guided = uncond + guidance * (cond - uncond)
    for g in range(row_groups):
        span = slice(g * PACK, (g + 1) * PACK)
        piece = guided[:, g * half:(g + 1) * half]
        latent = lat_in[span, :]
        next_ref[span, :] = latent + sigma_gain * piece
        clean_ref[span, :] = latent - sigma_now * piece

    whole_wait(recv2, 2 * group - 1, send2_sem)


def on_device(
    n,
    img_queries, img_keys, img_values, text_keys, text_values, query_gain, key_gain, text_gain,
    text_lengths, text_blocks, latent, base_velocity, out_weight, timestep,
):
    head_size = query_gain.shape[0]
    width = img_queries.shape[2]
    heads = width // head_size
    rows, texts = img_queries.shape[1], text_keys.shape[1]
    half = latent.shape[1]
    group = max(d for d in range(1, min(n, heads) + 1) if n % d == 0)
    plan = (n, group, heads, head_size, rows, texts, half)
    bf16, f32 = jnp.bfloat16, jnp.float32
    hbm = pl.BlockSpec(memory_space=pltpu.HBM)
    vmem = pl.BlockSpec(memory_space=pltpu.VMEM)
    smem = pl.BlockSpec(memory_space=pltpu.SMEM)
    return pl.pallas_call(
        functools.partial(exchange_kernel, plan),
        out_shape=[jax.ShapeDtypeStruct((rows, half), f32)] * 2,
        in_specs=[hbm] * 8 + [smem] * 2 + [hbm] * 3 + [smem],
        out_specs=[vmem] * 2,
        scratch_shapes=[
            pltpu.VMEM((rows, width), bf16),
            pltpu.VMEM((rows, width), bf16),
            pltpu.VMEM((rows, width), bf16),
            pltpu.VMEM((texts, width), bf16),
            pltpu.VMEM((texts, width), bf16),
            pltpu.VMEM((1, head_size), f32),
            pltpu.VMEM((1, head_size), f32),
            pltpu.VMEM((1, head_size), f32),
            pltpu.VMEM((rows, half), f32),
            pltpu.VMEM((rows, 2 * half), bf16),
            pltpu.VMEM((2 * half, width), bf16),
            pltpu.VMEM((heads, SLOT_ROWS, 256), bf16),
            pltpu.VMEM((2, n, SLOT_ROWS, 256), bf16),
            pltpu.VMEM((rows // PACK + 1, group * PACK, 128), f32),
            pltpu.VMEM((2, rows // PACK, 256, 128), bf16),
            pltpu.VMEM((2, group, PACK, 128), f32),
            pltpu.VMEM((2 * group, PACK, 128), f32),
            pltpu.SemaphoreType.DMA((11,)),
            pltpu.SemaphoreType.DMA((2,)),
            pltpu.SemaphoreType.DMA((2,)),
            pltpu.SemaphoreType.DMA,
            pltpu.SemaphoreType.DMA,
        ],
        compiler_params=pltpu.CompilerParams(
            collective_id=0, has_side_effects=True, vmem_limit_bytes=63 * 1024 * 1024
        ),
    )(
        img_queries, img_keys, img_values, text_keys, text_values,
        query_gain.reshape(1, -1), key_gain.reshape(1, -1), text_gain.reshape(1, -1),
        text_lengths, text_blocks, latent, base_velocity, out_weight.T, timestep,
    )


def solution(mesh):
    return jax.shard_map(
        functools.partial(on_device, mesh.shape["seq"]),
        mesh=mesh,
        in_specs=(
            P("cfg", "seq", None),
            P("cfg", "seq", None),
            P("cfg", "seq", None),
            P("cfg", "seq", None),
            P("cfg", "seq", None),
            P(),
            P(),
            P(),
            P("cfg"),
            P("cfg", "seq"),
            P("seq", "cfg"),
            P("cfg", "seq", None),
            P(),
            P(),
        ),
        out_specs=(P("seq", "cfg"), P("seq", "cfg")),
        check_vma=False,
    )
```

```python
import functools
import math

import jax
import jax.numpy as jnp
from jax import lax
from jax.experimental import pallas as pl
from jax.experimental.pallas import tpu as pltpu
from jax.sharding import PartitionSpec as P

STEPS = 28
MESH = pl.DeviceIdType.MESH

epsilon = 1e-06
guidance = 3.5
shift_factor = 3.0
masked_score = -1e30

SLOT_ROWS = 16
PACK = 4


def sigma_at(position):
    time_left = 1.0 - position / STEPS
    return shift_factor * time_left / (1.0 + (shift_factor - 1.0) * time_left)


def exchange_kernel(
    plan,
    q_hbm, k_hbm, v_hbm, tk_hbm, tv_hbm, gq_hbm, gk_hbm, gt_hbm, len_ref, blk_ref, lat_hbm, base_hbm, w_hbm, step_ref,
    out_ref,
    q_in, k_in, v_in, tk_in, tv_in, gq_ref, gk_ref, gt_ref, lat_in, base_in, w_in,
    stage, recv, packed, parts, recv2,
    load_sem, send_sem, recv_sem, send2_sem, recv2_sem,
):
    n, team, heads, head_size, rows, texts, half = plan
    row_groups = rows // PACK
    own_heads = heads // team
    extras = heads - own_heads * team
    slots = own_heads + (1 if extras else 0)
    stride = max(1, team // max(1, extras))
    if stride * (extras - 1) + 1 > team:
        stride = 1
    teams = n // team
    tile = SLOT_ROWS
    f32, bf16 = jnp.float32, jnp.bfloat16
    cfg = lax.axis_index("cfg")
    me = lax.axis_index("seq")
    place = lax.rem(me, team)
    first = me - place
    extra = jnp.minimum(lax.div(place, stride), max(extras - 1, 0))
    has_extra = (lax.rem(place, stride) == 0) & (lax.div(place, stride) < extras)
    extra_head = own_heads * team + extra

    def wrapped(value, size):
        return jnp.where(value >= size, value - size, value)

    def each_team(body):
        if teams <= 4:
            for t in range(1, teams):
                body(t)
        else:
            def step(t, carry):
                body(t)
                return carry
            lax.fori_loop(1, teams, step, 0)

    loads = []
    sources = (
        (k_hbm.at[0], k_in), (tk_hbm.at[0], tk_in), (q_hbm.at[0], q_in), (v_hbm.at[0], v_in), (tv_hbm.at[0], tv_in),
        (gq_hbm, gq_ref), (gk_hbm, gk_ref), (gt_hbm, gt_ref),
        (lat_hbm, lat_in), (base_hbm.at[0], base_in), (w_hbm, w_in),
    )
    for i, (src, dst) in enumerate(sources):
        load = pltpu.make_async_copy(src, dst, load_sem.at[i])
        load.start()
        loads.append(load)

    barrier = pltpu.get_barrier_semaphore()

    def greet(side, peer):
        pl.semaphore_signal(barrier, inc=1, device_id=(side, peer), device_id_type=MESH)

    def greet_team(t):
        other = wrapped(first + t * team, n)
        for i in range(team):
            greet(cfg, other + i)

    each_team(greet_team)
    for i in range(1, team):
        greet(cfg, first + wrapped(place + i, team))
    for i in range(team):
        greet(1 - cfg, first + i)

    lane = lax.broadcasted_iota(jnp.int32, (tile, 128), 1)
    row = lax.broadcasted_iota(jnp.int32, (tile, 128), 0)
    low = lane < head_size
    is_text = (row >= rows) & (row < rows + texts)
    is_flag = (lane == 0) & (row >= rows + texts) & (row < rows + 2 * texts)
    slot_index = me * texts + row - rows - texts
    flags = jnp.where(is_flag & (slot_index < len_ref[0]) & (blk_ref[0, 0] == 1), 1.0, 0.0)

    def chunk(ref, c):
        part = ref[:, c * 128:min((c + 1) * 128, heads * head_size)].astype(f32)
        if part.shape[1] < 128:
            part = jnp.concatenate([part, jnp.zeros((part.shape[0], 128 - part.shape[1]), f32)], axis=1)
        return part

    def tall(part):
        return jnp.concatenate([part, jnp.zeros((tile - part.shape[0], 128), f32)], axis=0)

    def with_text(part, text):
        if texts == 1:
            return jnp.where(row == rows, text, tall(part))
        return tall(jnp.concatenate([part, text], axis=0))

    def normed(part, gain):
        square = part * part
        left = jnp.sum(jnp.where(low, square, 0.0), axis=1, keepdims=True)
        right = jnp.sum(jnp.where(low, 0.0, square), axis=1, keepdims=True)
        mean = jnp.where(low, left, right) * (1.0 / head_size)
        return part * lax.rsqrt(mean + epsilon) * gain

    for load in loads[:8]:
        load.wait()
    gain_q = jnp.concatenate([gq_ref[...], gq_ref[...]], axis=1) * (1.0 / math.sqrt(head_size))
    gain_k = jnp.concatenate([gk_ref[...], gk_ref[...]], axis=1)
    gain_t = jnp.concatenate([gt_ref[...], gt_ref[...]], axis=1)
    gain_kt = jnp.where(is_text, gain_t, gain_k)
    for c in range((heads + 1) // 2):
        qn = normed(tall(chunk(q_in, c)), gain_q)
        kn = normed(with_text(chunk(k_in, c), chunk(tk_in, c)), gain_kt)
        vv = with_text(chunk(v_in, c), chunk(tv_in, c))
        q_turn = pltpu.roll(qn, head_size, 1)
        k_turn = pltpu.roll(kn, head_size, 1)
        v_turn = pltpu.roll(vv, head_size, 1)
        stage[2 * c, 0:tile] = (jnp.where(low, kn, v_turn) + flags).astype(bf16)
        stage[2 * c, tile:2 * tile] = jnp.where(low, qn, 0.0).astype(bf16)
        if 2 * c + 1 < heads:
            stage[2 * c + 1, 0:tile] = (jnp.where(low, k_turn, vv) + flags).astype(bf16)
            stage[2 * c + 1, tile:2 * tile] = jnp.where(low, q_turn, 0.0).astype(bf16)

    pl.semaphore_wait(barrier, n - 1 + team)

    def send(src, dst, kind, peer):
        pltpu.make_async_remote_copy(
            src_ref=src,
            dst_ref=dst,
            send_sem=send_sem.at[kind],
            recv_sem=recv_sem.at[kind],
            device_id=(cfg, peer),
            device_id_type=MESH,
        ).start()

    def send_team(t):
        other = wrapped(first + t * team, n)
        for e in range(extras):
            send(
                stage.at[own_heads * team + e, pl.ds(0, tile)], recv.at[me, own_heads, pl.ds(0, tile)],
                2, other + e * stride,
            )
        for i in range(team):
            p = wrapped(place + i, team)
            send(
                stage.at[pl.ds(p * own_heads, own_heads), pl.ds(0, tile)],
                recv.at[me, pl.ds(0, own_heads), pl.ds(0, tile)],
                0, other + p,
            )

    each_team(send_team)
    for e in range(extras):
        @pl.when(place != e * stride)
        def _():
            send(stage.at[own_heads * team + e], recv.at[me, own_heads], 3, first + e * stride)

    for i in range(1, team):
        p = wrapped(place + i, team)
        send(stage.at[pl.ds(p * own_heads, own_heads)], recv.at[me, pl.ds(0, own_heads)], 1, first + p)

    for j in range(own_heads):
        recv[me, j] = stage[place * own_heads + j]
    if extras:
        @pl.when(has_extra)
        def _():
            recv[me, own_heads] = stage[extra_head]

        @pl.when(jnp.logical_not(has_extra))
        def _():
            recv[:, own_heads] = jnp.zeros((n, 2 * tile, 128), bf16)

    for load in loads[8:]:
        load.wait()
    lane_w = lax.broadcasted_iota(jnp.int32, (2 * half, 128), 1)
    full = (heads * head_size) // 128
    head_weights = []
    for j in range(slots):
        head = place * own_heads + j if j < own_heads else extra_head
        pair = lax.div(head, 2)
        start = pl.multiple_of(jnp.minimum(pair, full - 1) * 128, 128)
        weight = w_in[:, pl.ds(start, 128)].astype(f32)
        if full * 128 < heads * head_size:
            weight = jnp.where(pair == full, chunk(w_in, full), weight)
        weight = jnp.where(lax.rem(head, 2) == 0, pltpu.roll(weight, head_size, 1), weight)
        head_weights.append(jnp.where(lane_w < head_size, 0.0, weight).astype(bf16))
    base = base_in[...].astype(f32)
    base_packed = []
    for side in range(2):
        pieces = [base[g * PACK:(g + 1) * PACK, side * half:(side + 1) * half] for g in range(row_groups)]
        pieces.append(jnp.zeros((PACK, 128 - row_groups * half), f32))
        base_packed.append(jnp.concatenate(pieces, axis=1))
    step_now = jnp.full((PACK, half), step_ref[0], jnp.int32).astype(f32)
    sigma_now = sigma_at(step_now)
    sigma_gain = sigma_at(step_now + 1.0) - sigma_now

    def whole_wait(span, sem):
        pltpu.make_async_copy(span, span, sem).wait()

    far = pl.ds(0, n - team)
    near = pl.ds(0, team - 1)
    whole_wait(recv.at[near, pl.ds(0, own_heads)], recv_sem.at[1])
    whole_wait(recv.at[far, pl.ds(0, own_heads), pl.ds(0, tile)], recv_sem.at[0])
    if extras:
        @pl.when(has_extra)
        def _():
            whole_wait(recv.at[near, own_heads], recv_sem.at[3])
            whole_wait(recv.at[far, own_heads, pl.ds(0, tile)], recv_sem.at[2])

    for s in range(team):
        for j in range(slots):
            own = recv[first + s, j, tile:2 * tile].astype(f32)
            for g in range(row_groups):
                at = (g * team + s) * PACK
                packed[j, at:at + PACK, :] = own[g * PACK:(g + 1) * PACK]

    nt = (((1,), (1,)), ((), ()))
    picker = jnp.where(lax.broadcasted_iota(jnp.int32, (8, 128), 1) == 0, 1.0, 0.0).astype(bf16)
    total = None
    bias = None
    for j in range(slots):
        pairs = recv[:, j, 0:tile].reshape(n * tile, 128)
        if bias is None:
            seen = lax.dot_general(picker, pairs, nt, preferred_element_type=f32)
            seen = pltpu.roll(seen, n * tile - texts, 1)[0:1]
            key_row = lax.rem(lax.broadcasted_iota(jnp.int32, (1, n * tile), 1), tile)
            open_key = (key_row < rows) | ((key_row < rows + texts) & (seen > 0.5))
            bias = jnp.where(open_key, 0.0, masked_score)
        scores = lax.dot_general(packed[j].astype(bf16), pairs, nt, preferred_element_type=f32) + bias
        top = jnp.max(scores, axis=1, keepdims=True)
        weights = jnp.exp(scores - top)
        den = jnp.sum(weights, axis=1, keepdims=True)
        num = jnp.dot(weights.astype(bf16), pairs, preferred_element_type=f32)
        attended = (num / den).astype(bf16)
        term = lax.dot_general(attended, head_weights[j], nt, preferred_element_type=f32)
        total = term if total is None else total + term

    span = team * PACK
    for side in range(2):
        pieces = [total[g * span:(g + 1) * span, side * half:(side + 1) * half] for g in range(row_groups)]
        pieces.append(jnp.zeros((span, 128 - row_groups * half), f32))
        block = jnp.concatenate(pieces, axis=1)
        for s in range(team):
            parts[side, s] = block[s * PACK:(s + 1) * PACK]
    for side in range(2):
        parts[side, place] = parts[side, place] + base_packed[side]

    mine = cfg * team + place

    def send_part(side, s):
        pltpu.make_async_remote_copy(
            src_ref=parts.at[side, s],
            dst_ref=recv2.at[mine],
            send_sem=send2_sem,
            recv_sem=recv2_sem,
            device_id=(side, first + s),
            device_id_type=MESH,
        ).start()

    for i in range(team):
        send_part(1 - cfg, wrapped(place + i, team))
    for i in range(1, team):
        send_part(cfg, wrapped(place + i, team))
    recv2[mine] = parts[cfg, place]

    whole_wait(recv.at[near, pl.ds(0, own_heads)], send_sem.at[1])
    whole_wait(recv.at[far, pl.ds(0, own_heads), pl.ds(0, tile)], send_sem.at[0])
    if extras:
        whole_wait(recv.at[pl.ds(0, extras * (teams - 1)), own_heads, pl.ds(0, tile)], send_sem.at[2])

        @pl.when(jnp.logical_not(has_extra))
        def _():
            whole_wait(recv.at[pl.ds(0, extras), own_heads], send_sem.at[3])
        if extras > 1:
            @pl.when(has_extra)
            def _():
                whole_wait(recv.at[pl.ds(0, extras - 1), own_heads], send_sem.at[3])

    whole_wait(recv2.at[pl.ds(0, 2 * team - 1)], recv2_sem)
    cond = jnp.sum(recv2[0:team], axis=0)
    uncond = jnp.sum(recv2[team:2 * team], axis=0)
    guided = uncond + guidance * (cond - uncond)
    for g in range(row_groups):
        at = slice(g * PACK, (g + 1) * PACK)
        piece = guided[:, g * half:(g + 1) * half]
        latent = lat_in[at, :]
        out_ref[0, at, :] = latent + sigma_gain * piece
        out_ref[1, at, :] = latent - sigma_now * piece

    whole_wait(recv2.at[pl.ds(0, 2 * team - 1)], send2_sem)


def on_device(
    n,
    img_queries, img_keys, img_values, text_keys, text_values, query_gain, key_gain, text_gain,
    text_lengths, text_blocks, latent, base_velocity, out_weight, timestep,
):
    head_size = query_gain.shape[0]
    width = img_queries.shape[2]
    heads = width // head_size
    rows, texts = img_queries.shape[1], text_keys.shape[1]
    half = latent.shape[1]
    team = max(d for d in range(1, min(n // 2, heads, 8) + 1) if n % d == 0)
    slots = -(-heads // team)
    plan = (n, team, heads, head_size, rows, texts, half)
    bf16, f32 = jnp.bfloat16, jnp.float32
    hbm = pl.BlockSpec(memory_space=pltpu.HBM)
    vmem = pl.BlockSpec(memory_space=pltpu.VMEM)
    smem = pl.BlockSpec(memory_space=pltpu.SMEM)
    both = pl.pallas_call(
        functools.partial(exchange_kernel, plan),
        out_shape=jax.ShapeDtypeStruct((2, rows, half), f32),
        in_specs=[hbm] * 8 + [smem] * 2 + [hbm] * 3 + [smem],
        out_specs=vmem,
        scratch_shapes=[
            pltpu.VMEM((rows, width), bf16),
            pltpu.VMEM((rows, width), bf16),
            pltpu.VMEM((rows, width), bf16),
            pltpu.VMEM((texts, width), bf16),
            pltpu.VMEM((texts, width), bf16),
            pltpu.VMEM((1, head_size), f32),
            pltpu.VMEM((1, head_size), f32),
            pltpu.VMEM((1, head_size), f32),
            pltpu.VMEM((rows, half), f32),
            pltpu.VMEM((rows, 2 * half), bf16),
            pltpu.VMEM((2 * half, width), bf16),
            pltpu.VMEM((heads, 2 * SLOT_ROWS, 128), bf16),
            pltpu.VMEM((n, slots, 2 * SLOT_ROWS, 128), bf16),
            pltpu.VMEM((slots, team * rows, 128), f32),
            pltpu.VMEM((2, team, PACK, 128), f32),
            pltpu.VMEM((2 * team, PACK, 128), f32),
            pltpu.SemaphoreType.DMA((11,)),
            pltpu.SemaphoreType.DMA((4,)),
            pltpu.SemaphoreType.DMA((4,)),
            pltpu.SemaphoreType.DMA,
            pltpu.SemaphoreType.DMA,
        ],
        compiler_params=pltpu.CompilerParams(
            collective_id=0, has_side_effects=True, vmem_limit_bytes=63 * 1024 * 1024
        ),
    )(
        img_queries, img_keys, img_values, text_keys, text_values,
        query_gain.reshape(1, -1), key_gain.reshape(1, -1), text_gain.reshape(1, -1),
        text_lengths, text_blocks, latent, base_velocity, out_weight.T, timestep,
    )
    return (both[0], both[1])


def solution(mesh):
    return jax.shard_map(
        functools.partial(on_device, mesh.shape["seq"]),
        mesh=mesh,
        in_specs=(
            P("cfg", "seq", None),
            P("cfg", "seq", None),
            P("cfg", "seq", None),
            P("cfg", "seq", None),
            P("cfg", "seq", None),
            P(),
            P(),
            P(),
            P("cfg"),
            P("cfg", "seq"),
            P("seq", "cfg"),
            P("cfg", "seq", None),
            P(),
            P(),
        ),
        out_specs=(P("seq", "cfg"), P("seq", "cfg")),
        check_vma=False,
    )
```

```python
import functools
import math

import jax
import jax.numpy as jnp
from jax import lax
from jax.experimental import pallas as pl
from jax.experimental.pallas import tpu as pltpu
from jax.sharding import PartitionSpec as P

STEPS = 28
MESH = pl.DeviceIdType.MESH

epsilon = 1e-06
guidance = 3.5
shift_factor = 3.0
masked_score = -1e30

SLOT_ROWS = 16
PACK = 4


def sigma_at(position):
    time_left = 1.0 - position / STEPS
    return shift_factor * time_left / (1.0 + (shift_factor - 1.0) * time_left)


def exchange_kernel(
    plan,
    q_hbm, k_hbm, v_hbm, tk_hbm, tv_hbm, gq_hbm, gk_hbm, gt_hbm, len_ref, blk_ref, lat_hbm, base_hbm, w_hbm, step_ref,
    out_ref,
    q_in, k_in, v_in, tk_in, tv_in, gq_ref, gk_ref, gt_ref, lat_in, base_in, w_in,
    stage, recv, packed, parts, recv2,
    load_sem, send_sem, recv_sem, send2_sem, recv2_sem,
):
    n, team, heads, head_size, rows, texts, half = plan
    row_groups = rows // PACK
    own_heads = heads // team
    extras = heads - own_heads * team
    slots = own_heads + (1 if extras else 0)
    stride = max(1, team // max(1, extras))
    if stride * (extras - 1) + 1 > team:
        stride = 1
    teams = n // team
    tile = SLOT_ROWS
    f32, bf16 = jnp.float32, jnp.bfloat16
    cfg = lax.axis_index("cfg")
    me = lax.axis_index("seq")
    place = lax.rem(me, team)
    first = me - place
    extra = jnp.minimum(lax.div(place, stride), max(extras - 1, 0))
    has_extra = (lax.rem(place, stride) == 0) & (lax.div(place, stride) < extras)
    extra_head = own_heads * team + extra

    def wrapped(value, size):
        return jnp.where(value >= size, value - size, value)

    def each_team(body):
        if teams <= 4:
            for t in range(1, teams):
                body(t)
        else:
            def step(t, carry):
                body(t)
                return carry
            lax.fori_loop(1, teams, step, 0)

    barrier = pltpu.get_barrier_semaphore()

    def greet(side, peer):
        pl.semaphore_signal(barrier, inc=1, device_id=(side, peer), device_id_type=MESH)

    def greet_team(t):
        other = wrapped(first + t * team, n)
        for i in range(team):
            greet(cfg, other + i)

    each_team(greet_team)
    for i in range(1, team):
        greet(cfg, first + wrapped(place + i, team))
    for i in range(team):
        greet(1 - cfg, first + i)

    loads = []
    sources = (
        (k_hbm.at[0], k_in), (tk_hbm.at[0], tk_in), (q_hbm.at[0], q_in), (v_hbm.at[0], v_in), (tv_hbm.at[0], tv_in),
        (gq_hbm, gq_ref), (gk_hbm, gk_ref), (gt_hbm, gt_ref),
        (lat_hbm, lat_in), (base_hbm.at[0], base_in), (w_hbm, w_in),
    )
    for i, (src, dst) in enumerate(sources):
        load = pltpu.make_async_copy(src, dst, load_sem.at[i])
        load.start()
        loads.append(load)

    lane = lax.broadcasted_iota(jnp.int32, (tile, 128), 1)
    row = lax.broadcasted_iota(jnp.int32, (tile, 128), 0)
    low = lane < head_size
    is_text = (row >= rows) & (row < rows + texts)
    is_flag = (lane == 0) & (row >= rows + texts) & (row < rows + 2 * texts)
    slot_index = me * texts + row - rows - texts
    flags = jnp.where(is_flag & (slot_index < len_ref[0]) & (blk_ref[0, 0] == 1), 1.0, 0.0)

    def chunk(ref, c):
        part = ref[:, c * 128:min((c + 1) * 128, heads * head_size)].astype(f32)
        if part.shape[1] < 128:
            part = jnp.concatenate([part, jnp.zeros((part.shape[0], 128 - part.shape[1]), f32)], axis=1)
        return part

    def tall(part):
        return jnp.concatenate([part, jnp.zeros((tile - part.shape[0], 128), f32)], axis=0)

    def with_text(part, text):
        if texts == 1:
            return jnp.where(row == rows, text, tall(part))
        return tall(jnp.concatenate([part, text], axis=0))

    def normed(part, gain):
        square = part * part
        left = jnp.sum(jnp.where(low, square, 0.0), axis=1, keepdims=True)
        right = jnp.sum(jnp.where(low, 0.0, square), axis=1, keepdims=True)
        mean = jnp.where(low, left, right) * (1.0 / head_size)
        return part * lax.rsqrt(mean + epsilon) * gain

    for load in loads[:8]:
        load.wait()
    gain_q = jnp.concatenate([gq_ref[...], gq_ref[...]], axis=1) * (1.0 / math.sqrt(head_size))
    gain_k = jnp.concatenate([gk_ref[...], gk_ref[...]], axis=1)
    gain_t = jnp.concatenate([gt_ref[...], gt_ref[...]], axis=1)
    gain_kt = jnp.where(is_text, gain_t, gain_k)
    for c in range((heads + 1) // 2):
        qn = normed(tall(chunk(q_in, c)), gain_q)
        kn = normed(with_text(chunk(k_in, c), chunk(tk_in, c)), gain_kt)
        vv = with_text(chunk(v_in, c), chunk(tv_in, c))
        q_turn = pltpu.roll(qn, head_size, 1)
        k_turn = pltpu.roll(kn, head_size, 1)
        v_turn = pltpu.roll(vv, head_size, 1)
        stage[2 * c, 0:tile] = (jnp.where(low, kn, v_turn) + flags).astype(bf16)
        stage[2 * c, tile:2 * tile] = jnp.where(low, qn, 0.0).astype(bf16)
        if 2 * c + 1 < heads:
            stage[2 * c + 1, 0:tile] = (jnp.where(low, k_turn, vv) + flags).astype(bf16)
            stage[2 * c + 1, tile:2 * tile] = jnp.where(low, q_turn, 0.0).astype(bf16)

    pl.semaphore_wait(barrier, n - 1 + team)

    def send(src, dst, kind, peer):
        pltpu.make_async_remote_copy(
            src_ref=src,
            dst_ref=dst,
            send_sem=send_sem.at[kind],
            recv_sem=recv_sem.at[kind],
            device_id=(cfg, peer),
            device_id_type=MESH,
        ).start()

    def send_team(t):
        other = wrapped(first + t * team, n)
        for e in range(extras):
            send(
                stage.at[own_heads * team + e, pl.ds(0, tile)], recv.at[me, own_heads, pl.ds(0, tile)],
                2, other + e * stride,
            )
        for i in range(team):
            p = wrapped(place + i, team)
            send(
                stage.at[pl.ds(p * own_heads, own_heads), pl.ds(0, tile)],
                recv.at[me, pl.ds(0, own_heads), pl.ds(0, tile)],
                0, other + p,
            )

    each_team(send_team)
    for e in range(extras):
        @pl.when(place != e * stride)
        def _():
            send(stage.at[own_heads * team + e], recv.at[me, own_heads], 3, first + e * stride)

    for i in range(1, team):
        p = wrapped(place + i, team)
        send(stage.at[pl.ds(p * own_heads, own_heads)], recv.at[me, pl.ds(0, own_heads)], 1, first + p)

    for j in range(own_heads):
        recv[me, j] = stage[place * own_heads + j]
    if extras:
        @pl.when(has_extra)
        def _():
            recv[me, own_heads] = stage[extra_head]

        @pl.when(jnp.logical_not(has_extra))
        def _():
            recv[:, own_heads] = jnp.zeros((n, 2 * tile, 128), bf16)

    for load in loads[8:]:
        load.wait()
    lane_w = lax.broadcasted_iota(jnp.int32, (2 * half, 128), 1)
    full = (heads * head_size) // 128
    head_weights = []
    for j in range(slots):
        head = place * own_heads + j if j < own_heads else extra_head
        pair = lax.div(head, 2)
        start = pl.multiple_of(jnp.minimum(pair, full - 1) * 128, 128)
        weight = w_in[:, pl.ds(start, 128)].astype(f32)
        if full * 128 < heads * head_size:
            weight = jnp.where(pair == full, chunk(w_in, full), weight)
        weight = jnp.where(lax.rem(head, 2) == 0, pltpu.roll(weight, head_size, 1), weight)
        head_weights.append(jnp.where(lane_w < head_size, 0.0, weight).astype(bf16))
    base = base_in[...].astype(f32)
    base_packed = []
    for side in range(2):
        pieces = [base[g * PACK:(g + 1) * PACK, side * half:(side + 1) * half] for g in range(row_groups)]
        pieces.append(jnp.zeros((PACK, 128 - row_groups * half), f32))
        base_packed.append(jnp.concatenate(pieces, axis=1))
    step_now = jnp.full((PACK, half), step_ref[0], jnp.int32).astype(f32)
    sigma_now = sigma_at(step_now)
    sigma_gain = sigma_at(step_now + 1.0) - sigma_now

    def whole_wait(span, sem):
        pltpu.make_async_copy(span, span, sem).wait()

    far = pl.ds(0, n - team)
    near = pl.ds(0, team - 1)
    whole_wait(recv.at[near, pl.ds(0, own_heads)], recv_sem.at[1])
    if extras:
        @pl.when(has_extra)
        def _():
            whole_wait(recv.at[near, own_heads], recv_sem.at[3])

    for s in range(team):
        for j in range(slots):
            own = recv[first + s, j, tile:2 * tile].astype(f32)
            for g in range(row_groups):
                at = (g * team + s) * PACK
                packed[j, at:at + PACK, :] = own[g * PACK:(g + 1) * PACK]

    nt = (((1,), (1,)), ((), ()))
    picker = jnp.where(lax.broadcasted_iota(jnp.int32, (8, 128), 1) == 0, 1.0, 0.0).astype(bf16)
    key_row = lax.rem(lax.broadcasted_iota(jnp.int32, (1, team * tile), 1), tile)

    def pairs_of(j, t):
        return recv[pl.ds(wrapped(first + t * team, n), team), j, 0:tile].reshape(team * tile, 128)

    def bias_of(t):
        seen = lax.dot_general(picker, pairs_of(0, t), nt, preferred_element_type=f32)
        seen = pltpu.roll(seen, team * tile - texts, 1)[0:1]
        open_key = (key_row < rows) | ((key_row < rows + texts) & (seen > 0.5))
        return jnp.where(open_key, 0.0, masked_score)

    queries = [packed[j].astype(bf16) for j in range(slots)]
    scores = [[] for j in range(slots)]
    for t in range(teams):
        if t == 1:
            whole_wait(recv.at[far, pl.ds(0, own_heads), pl.ds(0, tile)], recv_sem.at[0])
            if extras:
                @pl.when(has_extra)
                def _():
                    whole_wait(recv.at[far, own_heads, pl.ds(0, tile)], recv_sem.at[2])
        bias = bias_of(t)
        for j in range(slots):
            scores[j].append(lax.dot_general(queries[j], pairs_of(j, t), nt, preferred_element_type=f32) + bias)

    total = None
    for j in range(slots):
        top = functools.reduce(jnp.maximum, scores[j])
        top = jnp.max(top, axis=1, keepdims=True)
        weights = [jnp.exp(score - top) for score in scores[j]]
        den = jnp.sum(functools.reduce(jnp.add, weights), axis=1, keepdims=True)
        num = None
        for t in range(teams):
            term = jnp.dot(weights[t].astype(bf16), pairs_of(j, t), preferred_element_type=f32)
            num = term if num is None else num + term
        attended = (num / den).astype(bf16)
        term = lax.dot_general(attended, head_weights[j], nt, preferred_element_type=f32)
        total = term if total is None else total + term

    span = team * PACK
    for side in range(2):
        pieces = [total[g * span:(g + 1) * span, side * half:(side + 1) * half] for g in range(row_groups)]
        pieces.append(jnp.zeros((span, 128 - row_groups * half), f32))
        block = jnp.concatenate(pieces, axis=1)
        for s in range(team):
            parts[side, s] = block[s * PACK:(s + 1) * PACK]
    for side in range(2):
        parts[side, place] = parts[side, place] + base_packed[side]

    mine = cfg * team + place

    def send_part(side, s):
        pltpu.make_async_remote_copy(
            src_ref=parts.at[side, s],
            dst_ref=recv2.at[mine],
            send_sem=send2_sem,
            recv_sem=recv2_sem,
            device_id=(side, first + s),
            device_id_type=MESH,
        ).start()

    for i in range(team):
        send_part(1 - cfg, wrapped(place + i, team))
    for i in range(1, team):
        send_part(cfg, wrapped(place + i, team))
    recv2[mine] = parts[cfg, place]

    whole_wait(recv.at[near, pl.ds(0, own_heads)], send_sem.at[1])
    whole_wait(recv.at[far, pl.ds(0, own_heads), pl.ds(0, tile)], send_sem.at[0])
    if extras:
        whole_wait(recv.at[pl.ds(0, extras * (teams - 1)), own_heads, pl.ds(0, tile)], send_sem.at[2])

        @pl.when(jnp.logical_not(has_extra))
        def _():
            whole_wait(recv.at[pl.ds(0, extras), own_heads], send_sem.at[3])
        if extras > 1:
            @pl.when(has_extra)
            def _():
                whole_wait(recv.at[pl.ds(0, extras - 1), own_heads], send_sem.at[3])

    whole_wait(recv2.at[pl.ds(0, 2 * team - 1)], recv2_sem)
    cond = jnp.sum(recv2[0:team], axis=0)
    uncond = jnp.sum(recv2[team:2 * team], axis=0)
    guided = uncond + guidance * (cond - uncond)
    for g in range(row_groups):
        at = slice(g * PACK, (g + 1) * PACK)
        piece = guided[:, g * half:(g + 1) * half]
        latent = lat_in[at, :]
        out_ref[0, at, :] = latent + sigma_gain * piece
        out_ref[1, at, :] = latent - sigma_now * piece

    whole_wait(recv2.at[pl.ds(0, 2 * team - 1)], send2_sem)


def on_device(
    n,
    img_queries, img_keys, img_values, text_keys, text_values, query_gain, key_gain, text_gain,
    text_lengths, text_blocks, latent, base_velocity, out_weight, timestep,
):
    head_size = query_gain.shape[0]
    width = img_queries.shape[2]
    heads = width // head_size
    rows, texts = img_queries.shape[1], text_keys.shape[1]
    half = latent.shape[1]
    team = max(d for d in range(1, min(n // 2, heads, 8) + 1) if n % d == 0)
    slots = -(-heads // team)
    plan = (n, team, heads, head_size, rows, texts, half)
    bf16, f32 = jnp.bfloat16, jnp.float32
    hbm = pl.BlockSpec(memory_space=pltpu.HBM)
    vmem = pl.BlockSpec(memory_space=pltpu.VMEM)
    smem = pl.BlockSpec(memory_space=pltpu.SMEM)
    both = pl.pallas_call(
        functools.partial(exchange_kernel, plan),
        out_shape=pltpu.VMEM((2, rows, half), f32),
        in_specs=[hbm] * 8 + [smem] * 2 + [hbm] * 3 + [smem],
        out_specs=vmem,
        scratch_shapes=[
            pltpu.VMEM((rows, width), bf16),
            pltpu.VMEM((rows, width), bf16),
            pltpu.VMEM((rows, width), bf16),
            pltpu.VMEM((texts, width), bf16),
            pltpu.VMEM((texts, width), bf16),
            pltpu.VMEM((1, head_size), f32),
            pltpu.VMEM((1, head_size), f32),
            pltpu.VMEM((1, head_size), f32),
            pltpu.VMEM((rows, half), f32),
            pltpu.VMEM((rows, 2 * half), bf16),
            pltpu.VMEM((2 * half, width), bf16),
            pltpu.VMEM((heads, 2 * SLOT_ROWS, 128), bf16),
            pltpu.VMEM((n, slots, 2 * SLOT_ROWS, 128), bf16),
            pltpu.VMEM((slots, team * rows, 128), f32),
            pltpu.VMEM((2, team, PACK, 128), f32),
            pltpu.VMEM((2 * team, PACK, 128), f32),
            pltpu.SemaphoreType.DMA((11,)),
            pltpu.SemaphoreType.DMA((4,)),
            pltpu.SemaphoreType.DMA((4,)),
            pltpu.SemaphoreType.DMA,
            pltpu.SemaphoreType.DMA,
        ],
        compiler_params=pltpu.CompilerParams(
            collective_id=0, has_side_effects=True, vmem_limit_bytes=63 * 1024 * 1024
        ),
    )(
        img_queries, img_keys, img_values, text_keys, text_values,
        query_gain.reshape(1, -1), key_gain.reshape(1, -1), text_gain.reshape(1, -1),
        text_lengths, text_blocks, latent, base_velocity, out_weight.T, timestep,
    )
    return (both[0], both[1])


def solution(mesh):
    return jax.shard_map(
        functools.partial(on_device, mesh.shape["seq"]),
        mesh=mesh,
        in_specs=(
            P("cfg", "seq", None),
            P("cfg", "seq", None),
            P("cfg", "seq", None),
            P("cfg", "seq", None),
            P("cfg", "seq", None),
            P(),
            P(),
            P(),
            P("cfg"),
            P("cfg", "seq"),
            P("seq", "cfg"),
            P("cfg", "seq", None),
            P(),
            P(),
        ),
        out_specs=(P("seq", "cfg"), P("seq", "cfg")),
        check_vma=False,
    )
```

```python
import functools
import math

import jax
import jax.numpy as jnp
from jax import lax
from jax.experimental import pallas as pl
from jax.experimental.pallas import tpu as pltpu
from jax.sharding import PartitionSpec as P

STEPS = 28
MESH = pl.DeviceIdType.MESH

epsilon = 1e-06
guidance = 3.5
shift_factor = 3.0
masked_score = -1e30

SLOT_ROWS = 16
PACK = 4


def sigma_at(position):
    time_left = 1.0 - position / STEPS
    return shift_factor * time_left / (1.0 + (shift_factor - 1.0) * time_left)


def exchange_kernel(
    plan,
    q_hbm, k_hbm, v_hbm, tk_hbm, tv_hbm, gq_hbm, gk_hbm, gt_hbm, len_hbm, blk_hbm, lat_hbm, base_hbm, w_hbm, step_hbm,
    out_ref,
    q_in, k_in, v_in, tk_in, tv_in, gq_ref, gk_ref, gt_ref, len_ref, blk_ref, step_ref, lat_in, base_in, w_in,
    stage, recv, packed, parts, recv2,
    load_sem, send_sem, recv_sem, send2_sem, recv2_sem,
):
    n, team, heads, head_size, rows, texts, half = plan
    row_groups = rows // PACK
    own_heads = heads // team
    extras = heads - own_heads * team
    slots = own_heads + (1 if extras else 0)
    stride = max(1, team // max(1, extras))
    if stride * (extras - 1) + 1 > team:
        stride = 1
    teams = n // team
    tile = SLOT_ROWS
    f32, bf16 = jnp.float32, jnp.bfloat16
    cfg = lax.axis_index("cfg")
    me = lax.axis_index("seq")
    place = lax.rem(me, team)
    first = me - place
    extra = jnp.minimum(lax.div(place, stride), max(extras - 1, 0))
    has_extra = (lax.rem(place, stride) == 0) & (lax.div(place, stride) < extras)
    extra_head = own_heads * team + extra

    def wrapped(value, size):
        return jnp.where(value >= size, value - size, value)

    def each_team(body):
        if teams <= 4:
            for t in range(1, teams):
                body(t)
        else:
            def step(t, carry):
                body(t)
                return carry
            lax.fori_loop(1, teams, step, 0)

    barrier = pltpu.get_barrier_semaphore()

    def greet(side, peer):
        pl.semaphore_signal(barrier, inc=1, device_id=(side, peer), device_id_type=MESH)

    def greet_team(t):
        other = wrapped(first + t * team, n)
        for i in range(team):
            greet(cfg, other + i)

    each_team(greet_team)
    for i in range(1, team):
        greet(cfg, first + wrapped(place + i, team))
    for i in range(team):
        greet(1 - cfg, first + i)

    loads = []
    sources = (
        (k_hbm.at[0], k_in), (tk_hbm.at[0], tk_in), (q_hbm.at[0], q_in), (v_hbm.at[0], v_in), (tv_hbm.at[0], tv_in),
        (gq_hbm, gq_ref), (gk_hbm, gk_ref), (gt_hbm, gt_ref),
        (len_hbm, len_ref), (blk_hbm, blk_ref), (step_hbm, step_ref),
        (lat_hbm, lat_in), (base_hbm.at[0], base_in), (w_hbm, w_in),
    )
    for i, (src, dst) in enumerate(sources):
        load = pltpu.make_async_copy(src, dst, load_sem.at[i])
        load.start()
        loads.append(load)

    lane = lax.broadcasted_iota(jnp.int32, (tile, 128), 1)
    row = lax.broadcasted_iota(jnp.int32, (tile, 128), 0)
    low = lane < head_size
    is_text = (row >= rows) & (row < rows + texts)
    is_flag = (lane == 0) & (row >= rows + texts) & (row < rows + 2 * texts)
    slot_index = me * texts + row - rows - texts
    def chunk(ref, c):
        part = ref[:, c * 128:min((c + 1) * 128, heads * head_size)].astype(f32)
        if part.shape[1] < 128:
            part = jnp.concatenate([part, jnp.zeros((part.shape[0], 128 - part.shape[1]), f32)], axis=1)
        return part

    def tall(part):
        return jnp.concatenate([part, jnp.zeros((tile - part.shape[0], 128), f32)], axis=0)

    def with_text(part, text):
        if texts == 1:
            return jnp.where(row == rows, text, tall(part))
        return tall(jnp.concatenate([part, text], axis=0))

    def normed(part, gain):
        square = part * part
        left = jnp.sum(jnp.where(low, square, 0.0), axis=1, keepdims=True)
        right = jnp.sum(jnp.where(low, 0.0, square), axis=1, keepdims=True)
        mean = jnp.where(low, left, right) * (1.0 / head_size)
        return part * lax.rsqrt(mean + epsilon) * gain

    for load in loads[:10]:
        load.wait()
    usable = (slot_index < len_ref[...]) & (blk_ref[...] == 1)
    flags = jnp.where(is_flag & usable, 1.0, 0.0)
    gain_q = jnp.concatenate([gq_ref[...], gq_ref[...]], axis=1) * (1.0 / math.sqrt(head_size))
    gain_k = jnp.concatenate([gk_ref[...], gk_ref[...]], axis=1)
    gain_t = jnp.concatenate([gt_ref[...], gt_ref[...]], axis=1)
    gain_kt = jnp.where(is_text, gain_t, gain_k)
    for c in range((heads + 1) // 2):
        qn = normed(tall(chunk(q_in, c)), gain_q)
        kn = normed(with_text(chunk(k_in, c), chunk(tk_in, c)), gain_kt)
        vv = with_text(chunk(v_in, c), chunk(tv_in, c))
        q_turn = pltpu.roll(qn, head_size, 1)
        k_turn = pltpu.roll(kn, head_size, 1)
        v_turn = pltpu.roll(vv, head_size, 1)
        stage[2 * c, 0:tile] = (jnp.where(low, kn, v_turn) + flags).astype(bf16)
        stage[2 * c, tile:2 * tile] = jnp.where(low, qn, 0.0).astype(bf16)
        if 2 * c + 1 < heads:
            stage[2 * c + 1, 0:tile] = (jnp.where(low, k_turn, vv) + flags).astype(bf16)
            stage[2 * c + 1, tile:2 * tile] = jnp.where(low, q_turn, 0.0).astype(bf16)

    pl.semaphore_wait(barrier, n - 1 + team)

    def send(src, dst, kind, peer):
        pltpu.make_async_remote_copy(
            src_ref=src,
            dst_ref=dst,
            send_sem=send_sem.at[kind],
            recv_sem=recv_sem.at[kind],
            device_id=(cfg, peer),
            device_id_type=MESH,
        ).start()

    def send_team(t):
        other = wrapped(first + t * team, n)
        for e in range(extras):
            send(
                stage.at[own_heads * team + e, pl.ds(0, tile)], recv.at[me, own_heads, pl.ds(0, tile)],
                2, other + e * stride,
            )
        for i in range(team):
            p = wrapped(place + i, team)
            send(
                stage.at[pl.ds(p * own_heads, own_heads), pl.ds(0, tile)],
                recv.at[me, pl.ds(0, own_heads), pl.ds(0, tile)],
                0, other + p,
            )

    each_team(send_team)
    for e in range(extras):
        @pl.when(place != e * stride)
        def _():
            send(stage.at[own_heads * team + e], recv.at[me, own_heads], 3, first + e * stride)

    for i in range(1, team):
        p = wrapped(place + i, team)
        send(stage.at[pl.ds(p * own_heads, own_heads)], recv.at[me, pl.ds(0, own_heads)], 1, first + p)

    for j in range(own_heads):
        recv[me, j] = stage[place * own_heads + j]
    if extras:
        @pl.when(has_extra)
        def _():
            recv[me, own_heads] = stage[extra_head]

        @pl.when(jnp.logical_not(has_extra))
        def _():
            recv[:, own_heads] = jnp.zeros((n, 2 * tile, 128), bf16)

    for load in loads[10:]:
        load.wait()
    lane_w = lax.broadcasted_iota(jnp.int32, (2 * half, 128), 1)
    full = (heads * head_size) // 128
    head_weights = []
    for j in range(slots):
        head = place * own_heads + j if j < own_heads else extra_head
        pair = lax.div(head, 2)
        start = pl.multiple_of(jnp.minimum(pair, full - 1) * 128, 128)
        weight = w_in[:, pl.ds(start, 128)].astype(f32)
        if full * 128 < heads * head_size:
            weight = jnp.where(pair == full, chunk(w_in, full), weight)
        weight = jnp.where(lax.rem(head, 2) == 0, pltpu.roll(weight, head_size, 1), weight)
        head_weights.append(jnp.where(lane_w < head_size, 0.0, weight).astype(bf16))
    base = base_in[...].astype(f32)
    base_packed = []
    for side in range(2):
        pieces = [base[g * PACK:(g + 1) * PACK, side * half:(side + 1) * half] for g in range(row_groups)]
        pieces.append(jnp.zeros((PACK, 128 - row_groups * half), f32))
        base_packed.append(jnp.concatenate(pieces, axis=1))
    step_now = jnp.broadcast_to(step_ref[...], (PACK, half)).astype(f32)
    sigma_now = sigma_at(step_now)
    sigma_gain = sigma_at(step_now + 1.0) - sigma_now

    def whole_wait(span, sem):
        pltpu.make_async_copy(span, span, sem).wait()

    far = pl.ds(0, n - team)
    near = pl.ds(0, team - 1)
    whole_wait(recv.at[near, pl.ds(0, own_heads)], recv_sem.at[1])
    if extras:
        @pl.when(has_extra)
        def _():
            whole_wait(recv.at[near, own_heads], recv_sem.at[3])

    for s in range(team):
        for j in range(slots):
            own = recv[first + s, j, tile:2 * tile].astype(f32)
            for g in range(row_groups):
                at = (g * team + s) * PACK
                packed[j, at:at + PACK, :] = own[g * PACK:(g + 1) * PACK]

    nt = (((1,), (1,)), ((), ()))
    picker = jnp.where(lax.broadcasted_iota(jnp.int32, (8, 128), 1) == 0, 1.0, 0.0).astype(bf16)
    key_row = lax.rem(lax.broadcasted_iota(jnp.int32, (1, team * tile), 1), tile)

    def pairs_of(j, t):
        return recv[pl.ds(wrapped(first + t * team, n), team), j, 0:tile].reshape(team * tile, 128)

    def bias_of(t):
        seen = lax.dot_general(picker, pairs_of(0, t), nt, preferred_element_type=f32)
        seen = pltpu.roll(seen, team * tile - texts, 1)[0:1]
        open_key = (key_row < rows) | ((key_row < rows + texts) & (seen > 0.5))
        return jnp.where(open_key, 0.0, masked_score)

    queries = [packed[j].astype(bf16) for j in range(slots)]
    scores = [[] for j in range(slots)]
    for t in range(teams):
        if t == 1:
            whole_wait(recv.at[far, pl.ds(0, own_heads), pl.ds(0, tile)], recv_sem.at[0])
            if extras:
                @pl.when(has_extra)
                def _():
                    whole_wait(recv.at[far, own_heads, pl.ds(0, tile)], recv_sem.at[2])
        bias = bias_of(t)
        for j in range(slots):
            scores[j].append(lax.dot_general(queries[j], pairs_of(j, t), nt, preferred_element_type=f32) + bias)

    total = None
    for j in range(slots):
        top = functools.reduce(jnp.maximum, scores[j])
        top = jnp.max(top, axis=1, keepdims=True)
        weights = [jnp.exp(score - top) for score in scores[j]]
        den = jnp.sum(functools.reduce(jnp.add, weights), axis=1, keepdims=True)
        num = None
        for t in range(teams):
            term = jnp.dot(weights[t].astype(bf16), pairs_of(j, t), preferred_element_type=f32)
            num = term if num is None else num + term
        attended = (num / den).astype(bf16)
        term = lax.dot_general(attended, head_weights[j], nt, preferred_element_type=f32)
        total = term if total is None else total + term

    span = team * PACK
    for side in range(2):
        pieces = [total[g * span:(g + 1) * span, side * half:(side + 1) * half] for g in range(row_groups)]
        pieces.append(jnp.zeros((span, 128 - row_groups * half), f32))
        block = jnp.concatenate(pieces, axis=1)
        for s in range(team):
            parts[side, s] = block[s * PACK:(s + 1) * PACK]
    for side in range(2):
        parts[side, place] = parts[side, place] + base_packed[side]

    mine = cfg * team + place

    def send_part(side, s):
        pltpu.make_async_remote_copy(
            src_ref=parts.at[side, s],
            dst_ref=recv2.at[mine],
            send_sem=send2_sem,
            recv_sem=recv2_sem,
            device_id=(side, first + s),
            device_id_type=MESH,
        ).start()

    for i in range(team):
        send_part(1 - cfg, wrapped(place + i, team))
    for i in range(1, team):
        send_part(cfg, wrapped(place + i, team))
    recv2[mine] = parts[cfg, place]

    whole_wait(recv.at[near, pl.ds(0, own_heads)], send_sem.at[1])
    whole_wait(recv.at[far, pl.ds(0, own_heads), pl.ds(0, tile)], send_sem.at[0])
    if extras:
        whole_wait(recv.at[pl.ds(0, extras * (teams - 1)), own_heads, pl.ds(0, tile)], send_sem.at[2])

        @pl.when(jnp.logical_not(has_extra))
        def _():
            whole_wait(recv.at[pl.ds(0, extras), own_heads], send_sem.at[3])
        if extras > 1:
            @pl.when(has_extra)
            def _():
                whole_wait(recv.at[pl.ds(0, extras - 1), own_heads], send_sem.at[3])

    whole_wait(recv2.at[pl.ds(0, 2 * team - 1)], recv2_sem)
    cond = jnp.sum(recv2[0:team], axis=0)
    uncond = jnp.sum(recv2[team:2 * team], axis=0)
    guided = uncond + guidance * (cond - uncond)
    for g in range(row_groups):
        at = slice(g * PACK, (g + 1) * PACK)
        piece = guided[:, g * half:(g + 1) * half]
        latent = lat_in[at, :]
        out_ref[0, at, :] = latent + sigma_gain * piece
        out_ref[1, at, :] = latent - sigma_now * piece

    whole_wait(recv2.at[pl.ds(0, 2 * team - 1)], send2_sem)


def on_device(
    n,
    img_queries, img_keys, img_values, text_keys, text_values, query_gain, key_gain, text_gain,
    text_lengths, text_blocks, latent, base_velocity, out_weight, timestep,
):
    head_size = query_gain.shape[0]
    width = img_queries.shape[2]
    heads = width // head_size
    rows, texts = img_queries.shape[1], text_keys.shape[1]
    half = latent.shape[1]
    team = max(d for d in range(1, min(n // 2, heads, 8) + 1) if n % d == 0)
    slots = -(-heads // team)
    plan = (n, team, heads, head_size, rows, texts, half)
    bf16, f32 = jnp.bfloat16, jnp.float32
    hbm = pl.BlockSpec(memory_space=pltpu.HBM)
    vmem = pl.BlockSpec(memory_space=pltpu.VMEM)
    both = pl.pallas_call(
        functools.partial(exchange_kernel, plan),
        out_shape=pltpu.VMEM((2, rows, half), f32),
        in_specs=[hbm] * 14,
        out_specs=vmem,
        scratch_shapes=[
            pltpu.VMEM((rows, width), bf16),
            pltpu.VMEM((rows, width), bf16),
            pltpu.VMEM((rows, width), bf16),
            pltpu.VMEM((texts, width), bf16),
            pltpu.VMEM((texts, width), bf16),
            pltpu.VMEM((1, head_size), f32),
            pltpu.VMEM((1, head_size), f32),
            pltpu.VMEM((1, head_size), f32),
            pltpu.VMEM((1, 1), jnp.int32),
            pltpu.VMEM((1, 1), jnp.int32),
            pltpu.VMEM((1, 1), jnp.int32),
            pltpu.VMEM((rows, half), f32),
            pltpu.VMEM((rows, 2 * half), bf16),
            pltpu.VMEM((2 * half, width), bf16),
            pltpu.VMEM((heads, 2 * SLOT_ROWS, 128), bf16),
            pltpu.VMEM((n, slots, 2 * SLOT_ROWS, 128), bf16),
            pltpu.VMEM((slots, team * rows, 128), f32),
            pltpu.VMEM((2, team, PACK, 128), f32),
            pltpu.VMEM((2 * team, PACK, 128), f32),
            pltpu.SemaphoreType.DMA((14,)),
            pltpu.SemaphoreType.DMA((4,)),
            pltpu.SemaphoreType.DMA((4,)),
            pltpu.SemaphoreType.DMA,
            pltpu.SemaphoreType.DMA,
        ],
        compiler_params=pltpu.CompilerParams(
            collective_id=0, has_side_effects=True, vmem_limit_bytes=63 * 1024 * 1024
        ),
    )(
        img_queries, img_keys, img_values, text_keys, text_values,
        query_gain.reshape(1, -1), key_gain.reshape(1, -1), text_gain.reshape(1, -1),
        text_lengths.reshape(1, 1), text_blocks, latent, base_velocity, out_weight.T, timestep.reshape(1, 1),
    )
    return (both[0], both[1])


def solution(mesh):
    return jax.shard_map(
        functools.partial(on_device, mesh.shape["seq"]),
        mesh=mesh,
        in_specs=(
            P("cfg", "seq", None),
            P("cfg", "seq", None),
            P("cfg", "seq", None),
            P("cfg", "seq", None),
            P("cfg", "seq", None),
            P(),
            P(),
            P(),
            P("cfg"),
            P("cfg", "seq"),
            P("seq", "cfg"),
            P("cfg", "seq", None),
            P(),
            P(),
        ),
        out_specs=(P("seq", "cfg"), P("seq", "cfg")),
        check_vma=False,
    )
```

```python
import functools
import math

import jax
import jax.numpy as jnp
from jax import lax
from jax.experimental import pallas as pl
from jax.experimental.pallas import tpu as pltpu
from jax.sharding import PartitionSpec as P

STEPS = 28
MESH = pl.DeviceIdType.MESH

epsilon = 1e-06
guidance = 3.5
shift_factor = 3.0
masked_score = -1e30

SLOT_ROWS = 16
PACK = 4


def sigma_at(position):
    time_left = 1.0 - position / STEPS
    return shift_factor * time_left / (1.0 + (shift_factor - 1.0) * time_left)


def exchange_kernel(
    plan,
    q_hbm, k_hbm, v_hbm, tk_hbm, tv_hbm, gq_hbm, gk_hbm, gt_hbm, len_hbm, blk_hbm, lat_hbm, base_hbm, w_hbm, step_hbm,
    out_ref,
    q_in, k_in, v_in, tk_in, tv_in, gq_ref, gk_ref, gt_ref, len_ref, blk_ref, step_ref, lat_in, base_in, w_in,
    stage, recv, packed, parts, recv2,
    load_sem, send_sem, recv_sem, send2_sem, recv2_sem,
):
    n, team, heads, head_size, rows, texts, half = plan
    row_groups = rows // PACK
    own_heads = heads // team
    extras = heads - own_heads * team
    slots = own_heads + (1 if extras else 0)
    stride = max(1, team // max(1, extras))
    if stride * (extras - 1) + 1 > team:
        stride = 1
    teams = n // team
    tile = SLOT_ROWS
    f32, bf16 = jnp.float32, jnp.bfloat16
    cfg = lax.axis_index("cfg")
    me = lax.axis_index("seq")
    place = lax.rem(me, team)
    first = me - place
    extra = jnp.minimum(lax.div(place, stride), max(extras - 1, 0))
    has_extra = (lax.rem(place, stride) == 0) & (lax.div(place, stride) < extras)
    extra_head = own_heads * team + extra

    def wrapped(value, size):
        return jnp.where(value >= size, value - size, value)

    def rolled(start, stop, body):
        def step(i, carry):
            body(i)
            return carry
        lax.fori_loop(start, stop, step, 0)

    def each_team(body):
        if teams <= 4:
            for t in range(1, teams):
                body(t)
        else:
            def step(t, carry):
                body(t)
                return carry
            lax.fori_loop(1, teams, step, 0)

    barrier = pltpu.get_barrier_semaphore()

    def greet(side, peer):
        pl.semaphore_signal(barrier, inc=1, device_id=(side, peer), device_id_type=MESH)

    def greet_team(t):
        other = wrapped(first + t * team, n)
        rolled(0, team, lambda i: greet(cfg, other + i))

    each_team(greet_team)
    rolled(1, team, lambda i: greet(cfg, first + wrapped(place + i, team)))
    rolled(0, team, lambda i: greet(1 - cfg, first + i))

    loads = []
    sources = (
        (k_hbm.at[0], k_in), (tk_hbm.at[0], tk_in), (q_hbm.at[0], q_in), (v_hbm.at[0], v_in), (tv_hbm.at[0], tv_in),
        (gq_hbm, gq_ref), (gk_hbm, gk_ref), (gt_hbm, gt_ref),
        (len_hbm, len_ref), (blk_hbm, blk_ref), (step_hbm, step_ref),
        (lat_hbm, lat_in), (base_hbm.at[0], base_in), (w_hbm, w_in),
    )
    for i, (src, dst) in enumerate(sources):
        load = pltpu.make_async_copy(src, dst, load_sem.at[i])
        load.start()
        loads.append(load)

    lane = lax.broadcasted_iota(jnp.int32, (tile, 128), 1)
    row = lax.broadcasted_iota(jnp.int32, (tile, 128), 0)
    low = lane < head_size
    is_text = (row >= rows) & (row < rows + texts)
    is_flag = (lane == 0) & (row >= rows + texts) & (row < rows + 2 * texts)
    slot_index = me * texts + row - rows - texts
    def chunk(ref, c):
        part = ref[:, c * 128:min((c + 1) * 128, heads * head_size)].astype(f32)
        if part.shape[1] < 128:
            part = jnp.concatenate([part, jnp.zeros((part.shape[0], 128 - part.shape[1]), f32)], axis=1)
        return part

    def tall(part):
        return jnp.concatenate([part, jnp.zeros((tile - part.shape[0], 128), f32)], axis=0)

    def with_text(part, text):
        if texts == 1:
            return jnp.where(row == rows, text, tall(part))
        return tall(jnp.concatenate([part, text], axis=0))

    def normed(part, gain):
        square = part * part
        left = jnp.sum(jnp.where(low, square, 0.0), axis=1, keepdims=True)
        right = jnp.sum(jnp.where(low, 0.0, square), axis=1, keepdims=True)
        mean = jnp.where(low, left, right) * (1.0 / head_size)
        return part * lax.rsqrt(mean + epsilon) * gain

    for load in loads[:10]:
        load.wait()
    usable = (slot_index < len_ref[...]) & (blk_ref[...] == 1)
    flags = jnp.where(is_flag & usable, 1.0, 0.0)
    gain_q = jnp.concatenate([gq_ref[...], gq_ref[...]], axis=1) * (1.0 / math.sqrt(head_size))
    gain_k = jnp.concatenate([gk_ref[...], gk_ref[...]], axis=1)
    gain_t = jnp.concatenate([gt_ref[...], gt_ref[...]], axis=1)
    gain_kt = jnp.where(is_text, gain_t, gain_k)
    for c in range((heads + 1) // 2):
        qn = normed(tall(chunk(q_in, c)), gain_q)
        kn = normed(with_text(chunk(k_in, c), chunk(tk_in, c)), gain_kt)
        vv = with_text(chunk(v_in, c), chunk(tv_in, c))
        q_turn = pltpu.roll(qn, head_size, 1)
        k_turn = pltpu.roll(kn, head_size, 1)
        v_turn = pltpu.roll(vv, head_size, 1)
        stage[2 * c, 0:tile] = (jnp.where(low, kn, v_turn) + flags).astype(bf16)
        stage[2 * c, tile:2 * tile] = jnp.where(low, qn, 0.0).astype(bf16)
        if 2 * c + 1 < heads:
            stage[2 * c + 1, 0:tile] = (jnp.where(low, k_turn, vv) + flags).astype(bf16)
            stage[2 * c + 1, tile:2 * tile] = jnp.where(low, q_turn, 0.0).astype(bf16)

    pl.semaphore_wait(barrier, n - 1 + team)

    def send(src, dst, kind, peer):
        pltpu.make_async_remote_copy(
            src_ref=src,
            dst_ref=dst,
            send_sem=send_sem.at[kind],
            recv_sem=recv_sem.at[kind],
            device_id=(cfg, peer),
            device_id_type=MESH,
        ).start()

    def send_team(t):
        other = wrapped(first + t * team, n)
        for e in range(extras):
            send(
                stage.at[own_heads * team + e, pl.ds(0, tile)], recv.at[me, own_heads, pl.ds(0, tile)],
                2, other + e * stride,
            )

        def send_far(i):
            p = wrapped(place + i, team)
            send(
                stage.at[pl.ds(p * own_heads, own_heads), pl.ds(0, tile)],
                recv.at[me, pl.ds(0, own_heads), pl.ds(0, tile)],
                0, other + p,
            )

        rolled(0, team, send_far)

    each_team(send_team)
    for e in range(extras):
        @pl.when(place != e * stride)
        def _():
            send(stage.at[own_heads * team + e], recv.at[me, own_heads], 3, first + e * stride)

    def send_near(i):
        p = wrapped(place + i, team)
        send(stage.at[pl.ds(p * own_heads, own_heads)], recv.at[me, pl.ds(0, own_heads)], 1, first + p)

    rolled(1, team, send_near)

    for j in range(own_heads):
        recv[me, j] = stage[place * own_heads + j]
    if extras:
        @pl.when(has_extra)
        def _():
            recv[me, own_heads] = stage[extra_head]

        @pl.when(jnp.logical_not(has_extra))
        def _():
            recv[:, own_heads] = jnp.zeros((n, 2 * tile, 128), bf16)

    for load in loads[10:]:
        load.wait()
    lane_w = lax.broadcasted_iota(jnp.int32, (2 * half, 128), 1)
    full = (heads * head_size) // 128
    head_weights = []
    for j in range(slots):
        head = place * own_heads + j if j < own_heads else extra_head
        pair = lax.div(head, 2)
        start = pl.multiple_of(jnp.minimum(pair, full - 1) * 128, 128)
        weight = w_in[:, pl.ds(start, 128)].astype(f32)
        if full * 128 < heads * head_size:
            weight = jnp.where(pair == full, chunk(w_in, full), weight)
        weight = jnp.where(lax.rem(head, 2) == 0, pltpu.roll(weight, head_size, 1), weight)
        head_weights.append(jnp.where(lane_w < head_size, 0.0, weight).astype(bf16))
    base = base_in[...].astype(f32)
    base_packed = []
    for side in range(2):
        pieces = [base[g * PACK:(g + 1) * PACK, side * half:(side + 1) * half] for g in range(row_groups)]
        pieces.append(jnp.zeros((PACK, 128 - row_groups * half), f32))
        base_packed.append(jnp.concatenate(pieces, axis=1))
    step_now = jnp.broadcast_to(step_ref[...], (PACK, half)).astype(f32)
    sigma_now = sigma_at(step_now)
    sigma_gain = sigma_at(step_now + 1.0) - sigma_now

    def whole_wait(span, sem):
        pltpu.make_async_copy(span, span, sem).wait()

    far = pl.ds(0, n - team)
    near = pl.ds(0, team - 1)
    whole_wait(recv.at[near, pl.ds(0, own_heads)], recv_sem.at[1])
    if extras:
        @pl.when(has_extra)
        def _():
            whole_wait(recv.at[near, own_heads], recv_sem.at[3])

    for s in range(team):
        for j in range(slots):
            own = recv[first + s, j, tile:2 * tile].astype(f32)
            for g in range(row_groups):
                at = (g * team + s) * PACK
                packed[j, at:at + PACK, :] = own[g * PACK:(g + 1) * PACK]

    nt = (((1,), (1,)), ((), ()))
    picker = jnp.where(lax.broadcasted_iota(jnp.int32, (8, 128), 1) == 0, 1.0, 0.0).astype(bf16)
    key_row = lax.rem(lax.broadcasted_iota(jnp.int32, (1, team * tile), 1), tile)

    def pairs_of(j, t):
        return recv[pl.ds(wrapped(first + t * team, n), team), j, 0:tile].reshape(team * tile, 128)

    def bias_of(t):
        seen = lax.dot_general(picker, pairs_of(0, t), nt, preferred_element_type=f32)
        seen = pltpu.roll(seen, team * tile - texts, 1)[0:1]
        open_key = (key_row < rows) | ((key_row < rows + texts) & (seen > 0.5))
        return jnp.where(open_key, 0.0, masked_score)

    queries = [packed[j].astype(bf16) for j in range(slots)]
    scores = [[] for j in range(slots)]
    for t in range(teams):
        if t == 1:
            whole_wait(recv.at[far, pl.ds(0, own_heads), pl.ds(0, tile)], recv_sem.at[0])
            if extras:
                @pl.when(has_extra)
                def _():
                    whole_wait(recv.at[far, own_heads, pl.ds(0, tile)], recv_sem.at[2])
        bias = bias_of(t)
        for j in range(slots):
            scores[j].append(lax.dot_general(queries[j], pairs_of(j, t), nt, preferred_element_type=f32) + bias)

    total = None
    for j in range(slots):
        top = functools.reduce(jnp.maximum, scores[j])
        top = jnp.max(top, axis=1, keepdims=True)
        weights = [jnp.exp(score - top) for score in scores[j]]
        den = jnp.sum(functools.reduce(jnp.add, weights), axis=1, keepdims=True)
        num = None
        for t in range(teams):
            term = jnp.dot(weights[t].astype(bf16), pairs_of(j, t), preferred_element_type=f32)
            num = term if num is None else num + term
        attended = (num / den).astype(bf16)
        term = lax.dot_general(attended, head_weights[j], nt, preferred_element_type=f32)
        total = term if total is None else total + term

    span = team * PACK
    for side in range(2):
        pieces = [total[g * span:(g + 1) * span, side * half:(side + 1) * half] for g in range(row_groups)]
        pieces.append(jnp.zeros((span, 128 - row_groups * half), f32))
        block = jnp.concatenate(pieces, axis=1)
        for s in range(team):
            parts[side, s] = block[s * PACK:(s + 1) * PACK]
    for side in range(2):
        parts[side, place] = parts[side, place] + base_packed[side]

    mine = cfg * team + place

    def send_part(side, s):
        pltpu.make_async_remote_copy(
            src_ref=parts.at[side, s],
            dst_ref=recv2.at[mine],
            send_sem=send2_sem,
            recv_sem=recv2_sem,
            device_id=(side, first + s),
            device_id_type=MESH,
        ).start()

    rolled(0, team, lambda i: send_part(1 - cfg, wrapped(place + i, team)))
    rolled(1, team, lambda i: send_part(cfg, wrapped(place + i, team)))
    recv2[mine] = parts[cfg, place]

    whole_wait(recv.at[near, pl.ds(0, own_heads)], send_sem.at[1])
    whole_wait(recv.at[far, pl.ds(0, own_heads), pl.ds(0, tile)], send_sem.at[0])
    if extras:
        whole_wait(recv.at[pl.ds(0, extras * (teams - 1)), own_heads, pl.ds(0, tile)], send_sem.at[2])

        @pl.when(jnp.logical_not(has_extra))
        def _():
            whole_wait(recv.at[pl.ds(0, extras), own_heads], send_sem.at[3])
        if extras > 1:
            @pl.when(has_extra)
            def _():
                whole_wait(recv.at[pl.ds(0, extras - 1), own_heads], send_sem.at[3])

    whole_wait(recv2.at[pl.ds(0, 2 * team - 1)], recv2_sem)
    cond = jnp.sum(recv2[0:team], axis=0)
    uncond = jnp.sum(recv2[team:2 * team], axis=0)
    guided = uncond + guidance * (cond - uncond)
    for g in range(row_groups):
        at = slice(g * PACK, (g + 1) * PACK)
        piece = guided[:, g * half:(g + 1) * half]
        latent = lat_in[at, :]
        out_ref[0, at, :] = latent + sigma_gain * piece
        out_ref[1, at, :] = latent - sigma_now * piece

    whole_wait(recv2.at[pl.ds(0, 2 * team - 1)], send2_sem)


def on_device(
    n,
    img_queries, img_keys, img_values, text_keys, text_values, query_gain, key_gain, text_gain,
    text_lengths, text_blocks, latent, base_velocity, out_weight, timestep,
):
    head_size = query_gain.shape[0]
    width = img_queries.shape[2]
    heads = width // head_size
    rows, texts = img_queries.shape[1], text_keys.shape[1]
    half = latent.shape[1]
    team = max(d for d in range(1, min(n // 2, heads, 8) + 1) if n % d == 0)
    slots = -(-heads // team)
    plan = (n, team, heads, head_size, rows, texts, half)
    bf16, f32 = jnp.bfloat16, jnp.float32
    hbm = pl.BlockSpec(memory_space=pltpu.HBM)
    vmem = pl.BlockSpec(memory_space=pltpu.VMEM)
    both = pl.pallas_call(
        functools.partial(exchange_kernel, plan),
        out_shape=pltpu.VMEM((2, rows, half), f32),
        in_specs=[hbm] * 14,
        out_specs=vmem,
        scratch_shapes=[
            pltpu.VMEM((rows, width), bf16),
            pltpu.VMEM((rows, width), bf16),
            pltpu.VMEM((rows, width), bf16),
            pltpu.VMEM((texts, width), bf16),
            pltpu.VMEM((texts, width), bf16),
            pltpu.VMEM((1, head_size), f32),
            pltpu.VMEM((1, head_size), f32),
            pltpu.VMEM((1, head_size), f32),
            pltpu.VMEM((1, 1), jnp.int32),
            pltpu.VMEM((1, 1), jnp.int32),
            pltpu.VMEM((1, 1), jnp.int32),
            pltpu.VMEM((rows, half), f32),
            pltpu.VMEM((rows, 2 * half), bf16),
            pltpu.VMEM((2 * half, width), bf16),
            pltpu.VMEM((heads, 2 * SLOT_ROWS, 128), bf16),
            pltpu.VMEM((n, slots, 2 * SLOT_ROWS, 128), bf16),
            pltpu.VMEM((slots, team * rows, 128), f32),
            pltpu.VMEM((2, team, PACK, 128), f32),
            pltpu.VMEM((2 * team, PACK, 128), f32),
            pltpu.SemaphoreType.DMA((14,)),
            pltpu.SemaphoreType.DMA((4,)),
            pltpu.SemaphoreType.DMA((4,)),
            pltpu.SemaphoreType.DMA,
            pltpu.SemaphoreType.DMA,
        ],
        compiler_params=pltpu.CompilerParams(
            collective_id=0, has_side_effects=True, vmem_limit_bytes=63 * 1024 * 1024
        ),
    )(
        img_queries, img_keys, img_values, text_keys, text_values,
        query_gain.reshape(1, -1), key_gain.reshape(1, -1), text_gain.reshape(1, -1),
        text_lengths.reshape(1, 1), text_blocks, latent, base_velocity, out_weight.T, timestep.reshape(1, 1),
    )
    return (both[0], both[1])


def solution(mesh):
    return jax.shard_map(
        functools.partial(on_device, mesh.shape["seq"]),
        mesh=mesh,
        in_specs=(
            P("cfg", "seq", None),
            P("cfg", "seq", None),
            P("cfg", "seq", None),
            P("cfg", "seq", None),
            P("cfg", "seq", None),
            P(),
            P(),
            P(),
            P("cfg"),
            P("cfg", "seq"),
            P("seq", "cfg"),
            P("cfg", "seq", None),
            P(),
            P(),
        ),
        out_specs=(P("seq", "cfg"), P("seq", "cfg")),
        check_vma=False,
    )
```

```python
import functools
import math

import jax
import jax.numpy as jnp
from jax import lax
from jax.experimental import pallas as pl
from jax.experimental.pallas import tpu as pltpu
from jax.sharding import PartitionSpec as P

STEPS = 28
MESH = pl.DeviceIdType.MESH

epsilon = 1e-06
guidance = 3.5
shift_factor = 3.0
masked_score = -1e30

SLOT_ROWS = 16
PACK = 4


def sigma_at(position):
    time_left = 1.0 - position / STEPS
    return shift_factor * time_left / (1.0 + (shift_factor - 1.0) * time_left)


def exchange_kernel(
    plan,
    q_hbm, k_hbm, v_hbm, tk_hbm, tv_hbm, gq_hbm, gk_hbm, gt_hbm, len_hbm, blk_hbm, lat_hbm, base_hbm, w_hbm, step_hbm,
    out_ref,
    q_in, k_in, v_in, tk_in, tv_in, gq_ref, gk_ref, gt_ref, len_ref, blk_ref, step_ref, lat_in, base_in, w_in,
    stage, recv, packed, parts, recv2,
    load_sem, send_sem, recv_sem, send2_sem, recv2_sem,
):
    n, team, heads, head_size, rows, texts, half = plan
    row_groups = rows // PACK
    own_heads = heads // team
    extras = heads - own_heads * team
    slots = own_heads + (1 if extras else 0)
    stride = max(1, team // max(1, extras))
    if stride * (extras - 1) + 1 > team:
        stride = 1
    teams = n // team
    tile = SLOT_ROWS
    f32, bf16 = jnp.float32, jnp.bfloat16
    cfg = lax.axis_index("cfg")
    me = lax.axis_index("seq")
    place = lax.rem(me, team)
    first = me - place
    extra = jnp.minimum(lax.div(place, stride), max(extras - 1, 0))
    has_extra = (lax.rem(place, stride) == 0) & (lax.div(place, stride) < extras)
    extra_head = own_heads * team + extra

    def wrapped(value, size):
        return jnp.where(value >= size, value - size, value)

    def rolled(start, stop, body):
        def step(i, carry):
            body(i)
            return carry
        lax.fori_loop(start, stop, step, 0)

    def each_team(body):
        if teams <= 4:
            for t in range(1, teams):
                body(t)
        else:
            def step(t, carry):
                body(t)
                return carry
            lax.fori_loop(1, teams, step, 0)

    barrier = pltpu.get_barrier_semaphore()

    def greet(side, peer):
        pl.semaphore_signal(barrier, inc=1, device_id=(side, peer), device_id_type=MESH)

    def greet_team(t):
        other = wrapped(first + t * team, n)
        rolled(0, team, lambda i: greet(cfg, other + i))

    each_team(greet_team)
    rolled(1, team, lambda i: greet(cfg, first + wrapped(place + i, team)))
    rolled(0, team, lambda i: greet(1 - cfg, first + i))

    loads = []
    sources = (
        (k_hbm.at[0], k_in), (tk_hbm.at[0], tk_in), (q_hbm.at[0], q_in), (v_hbm.at[0], v_in), (tv_hbm.at[0], tv_in),
        (gq_hbm, gq_ref), (gk_hbm, gk_ref), (gt_hbm, gt_ref),
        (len_hbm, len_ref), (blk_hbm, blk_ref), (step_hbm, step_ref),
        (lat_hbm, lat_in), (base_hbm.at[0], base_in), (w_hbm, w_in),
    )
    for i, (src, dst) in enumerate(sources):
        load = pltpu.make_async_copy(src, dst, load_sem.at[i])
        load.start()
        loads.append(load)

    lane = lax.broadcasted_iota(jnp.int32, (tile, 128), 1)
    row = lax.broadcasted_iota(jnp.int32, (tile, 128), 0)
    low = lane < head_size
    is_text = (row >= rows) & (row < rows + texts)
    is_flag = (lane == 0) & (row >= rows + texts) & (row < rows + 2 * texts)
    slot_index = me * texts + row - rows - texts
    def chunk(ref, c):
        part = ref[:, c * 128:min((c + 1) * 128, heads * head_size)].astype(f32)
        if part.shape[1] < 128:
            part = jnp.concatenate([part, jnp.zeros((part.shape[0], 128 - part.shape[1]), f32)], axis=1)
        return part

    def tall(part):
        return jnp.concatenate([part, jnp.zeros((tile - part.shape[0], 128), f32)], axis=0)

    def with_text(part, text):
        if texts == 1:
            return jnp.where(row == rows, text, tall(part))
        return tall(jnp.concatenate([part, text], axis=0))

    def normed(part, gain):
        square = part * part
        left = jnp.sum(jnp.where(low, square, 0.0), axis=1, keepdims=True)
        right = jnp.sum(jnp.where(low, 0.0, square), axis=1, keepdims=True)
        mean = jnp.where(low, left, right) * (1.0 / head_size)
        return part * lax.rsqrt(mean + epsilon) * gain

    for load in loads[:10]:
        load.wait()
    usable = (slot_index < len_ref[...]) & (blk_ref[...] == 1)
    flags = jnp.where(is_flag & usable, 1.0, 0.0)
    gain_q = jnp.concatenate([gq_ref[...], gq_ref[...]], axis=1) * (1.0 / math.sqrt(head_size))
    gain_k = jnp.concatenate([gk_ref[...], gk_ref[...]], axis=1)
    gain_t = jnp.concatenate([gt_ref[...], gt_ref[...]], axis=1)
    gain_kt = jnp.where(is_text, gain_t, gain_k)
    for c in range((heads + 1) // 2):
        kn = normed(with_text(chunk(k_in, c), chunk(tk_in, c)), gain_kt)
        vv = with_text(chunk(v_in, c), chunk(tv_in, c))
        k_turn = pltpu.roll(kn, head_size, 1)
        v_turn = pltpu.roll(vv, head_size, 1)
        stage[2 * c, 0:tile] = (jnp.where(low, kn, v_turn) + flags).astype(bf16)
        if 2 * c + 1 < heads:
            stage[2 * c + 1, 0:tile] = (jnp.where(low, k_turn, vv) + flags).astype(bf16)

    pl.semaphore_wait(barrier, n - 1 + team)

    def send(src, dst, kind, peer):
        pltpu.make_async_remote_copy(
            src_ref=src,
            dst_ref=dst,
            send_sem=send_sem.at[kind],
            recv_sem=recv_sem.at[kind],
            device_id=(cfg, peer),
            device_id_type=MESH,
        ).start()

    def send_team(t):
        other = wrapped(first + t * team, n)
        for e in range(extras):
            send(
                stage.at[own_heads * team + e, pl.ds(0, tile)], recv.at[me, own_heads, pl.ds(0, tile)],
                2, other + e * stride,
            )

        def send_far(i):
            p = wrapped(place + i, team)
            send(
                stage.at[pl.ds(p * own_heads, own_heads), pl.ds(0, tile)],
                recv.at[me, pl.ds(0, own_heads), pl.ds(0, tile)],
                0, other + p,
            )

        rolled(0, team, send_far)

    each_team(send_team)
    for c in range((heads + 1) // 2):
        qn = normed(tall(chunk(q_in, c)), gain_q)
        stage[2 * c, tile:2 * tile] = jnp.where(low, qn, 0.0).astype(bf16)
        if 2 * c + 1 < heads:
            q_turn = pltpu.roll(qn, head_size, 1)
            stage[2 * c + 1, tile:2 * tile] = jnp.where(low, q_turn, 0.0).astype(bf16)
    for e in range(extras):
        @pl.when(place != e * stride)
        def _():
            send(stage.at[own_heads * team + e], recv.at[me, own_heads], 3, first + e * stride)

    def send_near(i):
        p = wrapped(place + i, team)
        send(stage.at[pl.ds(p * own_heads, own_heads)], recv.at[me, pl.ds(0, own_heads)], 1, first + p)

    rolled(1, team, send_near)

    for j in range(own_heads):
        recv[me, j] = stage[place * own_heads + j]
    if extras:
        @pl.when(has_extra)
        def _():
            recv[me, own_heads] = stage[extra_head]

        @pl.when(jnp.logical_not(has_extra))
        def _():
            recv[:, own_heads] = jnp.zeros((n, 2 * tile, 128), bf16)

    for load in loads[10:]:
        load.wait()
    lane_w = lax.broadcasted_iota(jnp.int32, (2 * half, 128), 1)
    full = (heads * head_size) // 128
    head_weights = []
    for j in range(slots):
        head = place * own_heads + j if j < own_heads else extra_head
        pair = lax.div(head, 2)
        start = pl.multiple_of(jnp.minimum(pair, full - 1) * 128, 128)
        weight = w_in[:, pl.ds(start, 128)].astype(f32)
        if full * 128 < heads * head_size:
            weight = jnp.where(pair == full, chunk(w_in, full), weight)
        weight = jnp.where(lax.rem(head, 2) == 0, pltpu.roll(weight, head_size, 1), weight)
        head_weights.append(jnp.where(lane_w < head_size, 0.0, weight).astype(bf16))
    base = base_in[...].astype(f32)
    base_packed = []
    for side in range(2):
        pieces = [base[g * PACK:(g + 1) * PACK, side * half:(side + 1) * half] for g in range(row_groups)]
        pieces.append(jnp.zeros((PACK, 128 - row_groups * half), f32))
        base_packed.append(jnp.concatenate(pieces, axis=1))
    step_now = jnp.broadcast_to(step_ref[...], (PACK, half)).astype(f32)
    sigma_now = sigma_at(step_now)
    sigma_gain = sigma_at(step_now + 1.0) - sigma_now

    def whole_wait(span, sem):
        pltpu.make_async_copy(span, span, sem).wait()

    far = pl.ds(0, n - team)
    near = pl.ds(0, team - 1)
    whole_wait(recv.at[near, pl.ds(0, own_heads)], recv_sem.at[1])
    if extras:
        @pl.when(has_extra)
        def _():
            whole_wait(recv.at[near, own_heads], recv_sem.at[3])

    for s in range(team):
        for j in range(slots):
            own = recv[first + s, j, tile:2 * tile].astype(f32)
            for g in range(row_groups):
                at = (g * team + s) * PACK
                packed[j, at:at + PACK, :] = own[g * PACK:(g + 1) * PACK]

    nt = (((1,), (1,)), ((), ()))
    picker = jnp.where(lax.broadcasted_iota(jnp.int32, (8, 128), 1) == 0, 1.0, 0.0).astype(bf16)
    key_row = lax.rem(lax.broadcasted_iota(jnp.int32, (1, team * tile), 1), tile)

    def pairs_of(j, t):
        return recv[pl.ds(wrapped(first + t * team, n), team), j, 0:tile].reshape(team * tile, 128)

    def bias_of(t):
        seen = lax.dot_general(picker, pairs_of(0, t), nt, preferred_element_type=f32)
        seen = pltpu.roll(seen, team * tile - texts, 1)[0:1]
        open_key = (key_row < rows) | ((key_row < rows + texts) & (seen > 0.5))
        return jnp.where(open_key, 0.0, masked_score)

    queries = [packed[j].astype(bf16) for j in range(slots)]
    scores = [[] for j in range(slots)]
    for t in range(teams):
        if t == 1:
            whole_wait(recv.at[far, pl.ds(0, own_heads), pl.ds(0, tile)], recv_sem.at[0])
            if extras:
                @pl.when(has_extra)
                def _():
                    whole_wait(recv.at[far, own_heads, pl.ds(0, tile)], recv_sem.at[2])
        bias = bias_of(t)
        for j in range(slots):
            scores[j].append(lax.dot_general(queries[j], pairs_of(j, t), nt, preferred_element_type=f32) + bias)

    total = None
    for j in range(slots):
        top = functools.reduce(jnp.maximum, scores[j])
        top = jnp.max(top, axis=1, keepdims=True)
        weights = [jnp.exp(score - top) for score in scores[j]]
        den = jnp.sum(functools.reduce(jnp.add, weights), axis=1, keepdims=True)
        num = None
        for t in range(teams):
            term = jnp.dot(weights[t].astype(bf16), pairs_of(j, t), preferred_element_type=f32)
            num = term if num is None else num + term
        attended = (num / den).astype(bf16)
        term = lax.dot_general(attended, head_weights[j], nt, preferred_element_type=f32)
        total = term if total is None else total + term

    span = team * PACK
    for side in range(2):
        pieces = [total[g * span:(g + 1) * span, side * half:(side + 1) * half] for g in range(row_groups)]
        pieces.append(jnp.zeros((span, 128 - row_groups * half), f32))
        block = jnp.concatenate(pieces, axis=1)
        for s in range(team):
            parts[side, s] = block[s * PACK:(s + 1) * PACK]
    for side in range(2):
        parts[side, place] = parts[side, place] + base_packed[side]

    mine = cfg * team + place

    def send_part(side, s):
        pltpu.make_async_remote_copy(
            src_ref=parts.at[side, s],
            dst_ref=recv2.at[mine],
            send_sem=send2_sem,
            recv_sem=recv2_sem,
            device_id=(side, first + s),
            device_id_type=MESH,
        ).start()

    rolled(0, team, lambda i: send_part(1 - cfg, wrapped(place + i, team)))
    rolled(1, team, lambda i: send_part(cfg, wrapped(place + i, team)))
    recv2[mine] = parts[cfg, place]

    whole_wait(recv.at[near, pl.ds(0, own_heads)], send_sem.at[1])
    whole_wait(recv.at[far, pl.ds(0, own_heads), pl.ds(0, tile)], send_sem.at[0])
    if extras:
        whole_wait(recv.at[pl.ds(0, extras * (teams - 1)), own_heads, pl.ds(0, tile)], send_sem.at[2])

        @pl.when(jnp.logical_not(has_extra))
        def _():
            whole_wait(recv.at[pl.ds(0, extras), own_heads], send_sem.at[3])
        if extras > 1:
            @pl.when(has_extra)
            def _():
                whole_wait(recv.at[pl.ds(0, extras - 1), own_heads], send_sem.at[3])

    whole_wait(recv2.at[pl.ds(0, 2 * team - 1)], recv2_sem)
    cond = jnp.sum(recv2[0:team], axis=0)
    uncond = jnp.sum(recv2[team:2 * team], axis=0)
    guided = uncond + guidance * (cond - uncond)
    for g in range(row_groups):
        at = slice(g * PACK, (g + 1) * PACK)
        piece = guided[:, g * half:(g + 1) * half]
        latent = lat_in[at, :]
        out_ref[0, at, :] = latent + sigma_gain * piece
        out_ref[1, at, :] = latent - sigma_now * piece

    whole_wait(recv2.at[pl.ds(0, 2 * team - 1)], send2_sem)


def on_device(
    n,
    img_queries, img_keys, img_values, text_keys, text_values, query_gain, key_gain, text_gain,
    text_lengths, text_blocks, latent, base_velocity, out_weight, timestep,
):
    head_size = query_gain.shape[0]
    width = img_queries.shape[2]
    heads = width // head_size
    rows, texts = img_queries.shape[1], text_keys.shape[1]
    half = latent.shape[1]
    team = max(d for d in range(1, min(n // 2, heads, 8) + 1) if n % d == 0)
    slots = -(-heads // team)
    plan = (n, team, heads, head_size, rows, texts, half)
    bf16, f32 = jnp.bfloat16, jnp.float32
    hbm = pl.BlockSpec(memory_space=pltpu.HBM)
    vmem = pl.BlockSpec(memory_space=pltpu.VMEM)
    both = pl.pallas_call(
        functools.partial(exchange_kernel, plan),
        out_shape=pltpu.VMEM((2, rows, half), f32),
        in_specs=[hbm] * 14,
        out_specs=vmem,
        scratch_shapes=[
            pltpu.VMEM((rows, width), bf16),
            pltpu.VMEM((rows, width), bf16),
            pltpu.VMEM((rows, width), bf16),
            pltpu.VMEM((texts, width), bf16),
            pltpu.VMEM((texts, width), bf16),
            pltpu.VMEM((1, head_size), f32),
            pltpu.VMEM((1, head_size), f32),
            pltpu.VMEM((1, head_size), f32),
            pltpu.VMEM((1, 1), jnp.int32),
            pltpu.VMEM((1, 1), jnp.int32),
            pltpu.VMEM((1, 1), jnp.int32),
            pltpu.VMEM((rows, half), f32),
            pltpu.VMEM((rows, 2 * half), bf16),
            pltpu.VMEM((2 * half, width), bf16),
            pltpu.VMEM((heads, 2 * SLOT_ROWS, 128), bf16),
            pltpu.VMEM((n, slots, 2 * SLOT_ROWS, 128), bf16),
            pltpu.VMEM((slots, team * rows, 128), f32),
            pltpu.VMEM((2, team, PACK, 128), f32),
            pltpu.VMEM((2 * team, PACK, 128), f32),
            pltpu.SemaphoreType.DMA((14,)),
            pltpu.SemaphoreType.DMA((4,)),
            pltpu.SemaphoreType.DMA((4,)),
            pltpu.SemaphoreType.DMA,
            pltpu.SemaphoreType.DMA,
        ],
        compiler_params=pltpu.CompilerParams(
            collective_id=0, has_side_effects=True, vmem_limit_bytes=63 * 1024 * 1024
        ),
    )(
        img_queries, img_keys, img_values, text_keys, text_values,
        query_gain.reshape(1, -1), key_gain.reshape(1, -1), text_gain.reshape(1, -1),
        text_lengths.reshape(1, 1), text_blocks, latent, base_velocity, out_weight.T, timestep.reshape(1, 1),
    )
    return (both[0], both[1])


def solution(mesh):
    return jax.shard_map(
        functools.partial(on_device, mesh.shape["seq"]),
        mesh=mesh,
        in_specs=(
            P("cfg", "seq", None),
            P("cfg", "seq", None),
            P("cfg", "seq", None),
            P("cfg", "seq", None),
            P("cfg", "seq", None),
            P(),
            P(),
            P(),
            P("cfg"),
            P("cfg", "seq"),
            P("seq", "cfg"),
            P("cfg", "seq", None),
            P(),
            P(),
        ),
        out_specs=(P("seq", "cfg"), P("seq", "cfg")),
        check_vma=False,
    )
```
